32 devices in a mesh: sec: 4 (over x, core), ctx: 8 (over z, y).
Axes of the slice: x: 2, y: 2, z: 4, core: 2. Of those that a mesh axis runs over, the one named last changes fastest.
Arguments:
- queries: bfloat16 [4, 16, 64, 4096], P('sec', 'ctx'), may hold values from -6 to 6
- head_weights: float32 [4, 16, 64, 32], P('sec', 'ctx'), may hold values from -0.9 to 0.9
- key_vectors: bfloat16 [4, 65536, 128], P('sec', 'ctx'), may hold values from -6 to 6
- targets: bfloat16 [4, 16, 64, 4096], P('sec', 'ctx'), may hold values from 0 to 0.0019989014
- normalizers: float32 [4, 16, 64], P('sec', 'ctx'), may hold values from 7 to 9
- loss_grad: float32 [4, 16, 64], P('sec', 'ctx'), may hold values from 300 to 3000
- tile_slot: int32 [4, 16], P('sec', 'ctx'), may hold values from 0 to 127
- doc_start: int32 [4, 16], P('sec', 'ctx'), may hold values from 0 to 65535, as said below
Outputs:
- queries_grad: bfloat16 [4, 16, 64, 4096], P('sec', 'ctx')
- weights_grad: float32 [4, 16, 64, 32], P('sec', 'ctx')
- key_grads: bfloat16 [4, 65536, 128], P('sec', 'ctx')
The draws below stay inside these ranges and needn't reach their ends.
Inputs may be any that keep to these rules, and one draw needn't show every extreme that they name: `doc_start`: qpos of every task lies in its device's positions; the document of a task starts at or before its first query and spans 1 to 4 key blocks up to its last query; the first task of every device but the first spans 4 blocks and its document starts on the device before.
All inputs are finite; a program needn't handle non-finite values.
Results may differ from the reference program's by a relative error of at most 0.0051.
Values may be sent and summed in bfloat16 or wider, within the bound.
No kernel may reach another device: no remote copies, remote signals or barrier semaphores. Data moves between devices by JAX's collectives and lax.ppermute only.
A program may use at most 192 MiB of HBM per device.

```python
import math
import jax
import jax.numpy as jnp
from jax import lax

H = 32
DH = 128
BLK = 1024
MAXB = 4
QT = 64
TASK_DEV = 2
KB_DEV = 8
SEQS = 4
NTASK = 16
SEQ = 65536


def task_layout(key):
    base = jax.random.fold_in(key, 7103)
    keys_list = jax.random.split(base, 4)
    shape_pair = (SEQS, NTASK)
    task_ids = jnp.arange(NTASK, dtype=jnp.int32)[None, :] + jnp.zeros(shape_pair, jnp.int32)
    device_ids = task_ids // TASK_DEV
    crossing = (task_ids % TASK_DEV == 0) & (device_ids > 0)
    free_block = jax.random.randint(keys_list[0], shape_pair, 0, KB_DEV)
    cross_block = jax.random.randint(keys_list[1], shape_pair, 0, MAXB - 1)
    local_block = jnp.where(crossing, cross_block, free_block)
    per_block = BLK // QT
    within = jax.random.randint(keys_list[2], shape_pair, 0, per_block)
    slot_value = local_block * per_block + within
    free_back = jax.random.randint(keys_list[3], shape_pair, 0, MAXB)
    back_blocks = jnp.where(crossing, MAXB - 1, free_back)
    last_block = device_ids * KB_DEV + local_block
    first_block = jnp.maximum(last_block - back_blocks, 0)
    query_first = last_block * BLK + within * QT
    span = jnp.minimum(BLK, query_first - first_block * BLK + 1)
    offset = jax.random.randint(jax.random.fold_in(base, 11), shape_pair, 0, 1 << 20) % span
    doc_begin = first_block * BLK + offset
    return (slot_value.astype(jnp.int32), doc_begin.astype(jnp.int32))


def draw_tile_slot(key, part):
    return task_layout(key)[0]


def draw_doc_start(key, part):
    return task_layout(key)[1]


def steps_of(own_key, dims, cuts, least, high):
    def one(dim, shards_of):
        heights = jax.random.uniform(jax.random.fold_in(jax.random.fold_in(own_key, 6), dim), (shards_of,), jnp.float32, least / len(cuts), high / len(cuts))
        return jnp.repeat(jnp.exp(heights), dims[dim] // shards_of).reshape((-1,) + (1,) * (len(dims) - dim - 1))

    factor_of = one(*cuts[0])
    for cut in cuts[1:]:
        factor_of = factor_of * one(*cut)
    return factor_of


def gaussian(stream_key, shape, spread, limit, shards=(), kind=jnp.bfloat16):
    factor_of = steps_of(stream_key, shape, shards, -0.22, 0.18) if shards else 1.0
    drawn = jax.random.normal(stream_key, shape, jnp.float32) * spread * factor_of
    return jnp.minimum(jnp.maximum(drawn, -limit), limit).astype(kind)


def setup_inputs(seed: int = 0) -> dict:
    key_of = jax.random.split(jax.random.key(seed), 9)
    return {
        "queries": gaussian(key_of[0], (SEQS, NTASK, QT, H * DH), 1.0, 6.0, ((0, 4), (1, 8))),
        "head_weights": gaussian(key_of[1], (SEQS, NTASK, QT, H), 0.15, 0.9, ((0, 4), (1, 8)), jnp.float32),
        "key_vectors": gaussian(key_of[2], (SEQS, SEQ, DH), 1.0, 6.0, ((0, 4), (1, 8))),
        "targets": jnp.clip(0.0019989014 * jax.random.uniform(key_of[3], (SEQS, NTASK, QT, MAXB * BLK), jnp.float32) ** steps_of(key_of[3], (SEQS, NTASK, QT, MAXB * BLK), ((0, 4), (1, 8)), -0.2, 0.2), 0.0, 0.0019989014).astype(jnp.bfloat16),
        "normalizers": jnp.clip(7.0 + 2.0 * jax.random.uniform(key_of[4], (SEQS, NTASK, QT), jnp.float32) ** steps_of(key_of[4], (SEQS, NTASK, QT), ((0, 4), (1, 8)), -0.2, 0.2), 7.0, 9.0),
        "loss_grad": jnp.clip(jnp.exp(math.log(3000.0) - 2.3025851 * jax.random.uniform(key_of[5], (SEQS, NTASK, QT), jnp.float32) ** steps_of(key_of[5], (SEQS, NTASK, QT), ((0, 4), (1, 8)), -0.2, 0.2)), 300.0, 3000.0),
        "tile_slot": draw_tile_slot(jax.random.fold_in(key_of[8], 71), 0),
        "doc_start": draw_doc_start(jax.random.fold_in(key_of[8], 71), 0),
    }


def block_terms(query_rows, weight_rows, normalizer, cotangent, target_block, key_block, key_first, query_pos, doc_begin, inside):
    tile_rows = weight_rows.shape[0]
    head_count = weight_rows.shape[1]
    block_width = key_block.shape[0]
    factor = 1.0 / (key_block.shape[1] ** 0.5)
    scores = lax.dot_general(query_rows, key_block, (((1,), (1,)), ((), ())), preferred_element_type=jnp.float32)
    scores = scores.reshape(tile_rows, head_count, block_width)
    active = jnp.maximum(scores, 0.0) * factor
    index_value = jnp.sum(weight_rows[:, :, None] * active, axis=1)
    key_pos = key_first + jnp.arange(block_width, dtype=jnp.int32)
    live = (key_pos[None, :] >= doc_begin) & (key_pos[None, :] <= query_pos[:, None]) & inside
    delta = jnp.where(live, cotangent[:, None] * (jnp.exp(index_value - normalizer[:, None]) - target_block.astype(jnp.float32)), 0.0)
    weight_part = jnp.sum(delta[:, None, :] * active, axis=2)
    score_grad = jnp.where(scores > 0, delta[:, None, :] * weight_rows[:, :, None] * factor, 0.0).astype(jnp.bfloat16)
    score_grad = score_grad.reshape(tile_rows * head_count, block_width)
    query_part = jnp.dot(score_grad, key_block, preferred_element_type=jnp.float32)
    key_part = lax.dot_general(score_grad, query_rows, (((0,), (0,)), ((), ())), preferred_element_type=jnp.float32)
    return query_part, weight_part, key_part


def one_sequence(operands):
    queries, head_weights, key_vectors, targets, normalizers, loss_grad, tile_slot, doc_start = operands

    def one_task(key_state, task_items):
        task_index, query_tile, weight_rows, target_rows, normalizer, cotangent, slot_value, doc_begin = task_items
        query_rows = query_tile.reshape(QT * H, DH)
        query_first = (task_index // TASK_DEV) * (KB_DEV * BLK) + slot_value * QT
        query_pos = query_first + jnp.arange(QT, dtype=jnp.int32)
        first_block = doc_begin // BLK
        block_count = (query_first + QT - 1) // BLK - first_block + 1

        def per_slot(slot_index, carry):
            query_total, weight_total, own_sum, lent_sum = carry
            block_id = first_block + slot_index
            key_block = lax.dynamic_slice_in_dim(key_vectors, (block_id * BLK).astype(jnp.int32), BLK, 0)
            target_block = lax.dynamic_slice_in_dim(target_rows, (slot_index * BLK).astype(jnp.int32), BLK, 1)
            query_part, weight_part, key_part = block_terms(query_rows, weight_rows, normalizer, cotangent, target_block, key_block, block_id * BLK, query_pos, doc_begin, True)
            is_own = (block_id // KB_DEV) == (task_index // TASK_DEV)
            start = (block_id * BLK).astype(jnp.int32)
            prev_own = lax.dynamic_slice_in_dim(own_sum, start, BLK, 0)
            own_sum = lax.dynamic_update_slice_in_dim(own_sum, prev_own + jnp.where(is_own, key_part, 0.0), start, 0)
            prev_lent = lax.dynamic_slice_in_dim(lent_sum, start, BLK, 0)
            lent_sum = lax.dynamic_update_slice_in_dim(lent_sum, prev_lent + jnp.where(is_own, 0.0, key_part), start, 0)
            return query_total + query_part, weight_total + weight_part, own_sum, lent_sum

        start_state = (jnp.zeros((QT * H, DH), jnp.float32), jnp.zeros((QT, H), jnp.float32), key_state[0], key_state[1])
        query_total, weight_total, own_sum, lent_sum = lax.fori_loop(0, block_count, per_slot, start_state)
        return (own_sum, lent_sum), (query_total.reshape(QT, H * DH).astype(jnp.bfloat16), weight_total)

    key_start = (jnp.zeros((SEQ, DH), jnp.float32), jnp.zeros((SEQ, DH), jnp.float32))
    task_ids = jnp.arange(NTASK, dtype=jnp.int32)
    key_state, outputs = lax.scan(one_task, key_start, (task_ids, queries, head_weights, targets, normalizers, loss_grad, tile_slot, doc_start))
    lent_round = lax.optimization_barrier(key_state[1].astype(jnp.bfloat16))
    key_out = (key_state[0] + lent_round.astype(jnp.float32)).astype(jnp.bfloat16)
    return outputs[0], outputs[1], key_out


def reference(queries, head_weights, key_vectors, targets, normalizers, loss_grad, tile_slot, doc_start):
    query_out, weight_out, key_out = lax.map(one_sequence, (queries, head_weights, key_vectors, targets, normalizers, loss_grad, tile_slot, doc_start))
    return query_out, weight_out, key_out
```

```python
import functools

import jax
import jax.numpy as jnp
from jax import lax
from jax.experimental import pallas as pl
from jax.experimental.pallas import tpu as pltpu
from jax.sharding import PartitionSpec as P

BLK = 1024
MAXB = 4
RIM = (MAXB - 1) * BLK
HALF = RIM // 2
WIDTH = 512
GROUP = 8
LANES = 128
DOWN = 2.0**-16
UP = 2.0**16
PRE_CHUNKS = 100
PIECE_CHUNKS = 0

f32 = jnp.float32
bf16 = jnp.bfloat16


def passed_along(array, by):
    size = lax.axis_size("ctx")
    pairs = [(i, i + by) for i in range(size) if 0 <= i + by < size]
    return lax.ppermute(array, "ctx", pairs)


def task_spans(slot_ref, doc_ref, tile_rows, regions):
    base = lax.axis_index("ctx") * (regions["own"][1] - RIM) - RIM
    tasks = []
    for i in range(doc_ref.shape[1]):
        doc = doc_ref[0, i] - base
        query = slot_ref[0, i] * tile_rows + RIM
        block = doc // BLK * BLK
        spans = {}
        for name, (start, stop) in regions.items():
            low = jnp.maximum(doc // LANES * LANES, start)
            high = jnp.minimum(query + tile_rows, stop)
            count = jnp.maximum(high - low + WIDTH - 1, 0) // WIDTH
            last = jnp.minimum(stop, block + MAXB * BLK) - WIDTH
            spans[name] = (low, count, last)
        tasks.append((doc, query, block, spans))
    return tasks


def pick(index, values):
    out = values[0]
    for i in range(1, len(values)):
        out = jnp.where(index == i, values[i], out)
    return out


def chunk_loop(tasks, name, begin, end, st):
    q2, wqt, wb, nm, ct, tg, keys, dq, dk, rb = st
    head_rows = q2.shape[1]
    tile_rows = nm.shape[1]
    rows = GROUP * tile_rows
    depth = q2.shape[2]
    lows = [t[3][name][0] for t in tasks]
    counts = [t[3][name][1] for t in tasks]
    lasts = [t[3][name][2] for t in tasks]
    factor = DOWN / depth**0.5

    def body(o, carry):
        task = jnp.int32(0)
        before = jnp.int32(0)
        seen = jnp.int32(0)
        for i in range(1, len(tasks)):
            seen = seen + counts[i - 1]
            task = jnp.where(o >= seen, i, task)
            before = jnp.where(o >= seen, seen, before)
        first = pick(task, lows) + (o - before) * WIDTH
        start = jnp.minimum(first, pick(task, lasts))
        start = pl.multiple_of(jnp.clip(start, 0, keys.shape[0] - WIDTH), LANES)
        column = start - pick(task, [t[2] for t in tasks])
        column = pl.multiple_of(jnp.clip(column, 0, tg.shape[2] - WIDTH), LANES)
        low = jnp.maximum(first, pick(task, [t[0] for t in tasks]))
        query = pick(task, [t[1] for t in tasks])
        span = pl.ds(start, WIDTH)
        key = keys[span, :]
        index = jnp.zeros((tile_rows, WIDTH), f32)
        for g in range(head_rows // rows):
            s = lax.dot_general(
                q2[task, g * rows : (g + 1) * rows, :],
                key,
                (((1,), (1,)), ((), ())),
                preferred_element_type=f32,
            )
            r = jnp.maximum(s, 0.0)
            for u in range(GROUP):
                w = wb[task, g * rows + u * tile_rows : g * rows + (u + 1) * tile_rows, :]
                w = jnp.concatenate([w] * (WIDTH // LANES), axis=1)
                index = index + w * r[u * tile_rows : (u + 1) * tile_rows]
            rb[g * rows : (g + 1) * rows, :] = r.astype(bf16)
        wide = [1, WIDTH // LANES]
        norm = jnp.concatenate([nm[task]] * wide[1], axis=1)
        cot = jnp.concatenate([ct[task]] * wide[1], axis=1)
        target = tg[task, :, pl.ds(column, WIDTH)].astype(f32)
        key_row = start + lax.broadcasted_iota(jnp.int32, (tile_rows, WIDTH), 1)
        query_row = query + lax.broadcasted_iota(jnp.int32, (tile_rows, WIDTH), 0)
        live = (key_row >= low) & (key_row <= query_row)
        delta = jnp.where(live, cot * (jnp.exp(index - norm) - target) * factor, 0.0)
        delta = jnp.concatenate([delta.astype(bf16)] * GROUP, axis=0)
        key_sum = None
        for g in range(head_rows // rows):
            here = slice(g * rows, (g + 1) * rows)
            grad = jnp.where(rb[here, :] > 0, delta, jnp.zeros_like(delta))
            dq[task, here, :] += jnp.dot(grad, key, preferred_element_type=f32)
            part = jnp.dot(wqt[task, :, here], grad, preferred_element_type=f32)
            key_sum = part if key_sum is None else key_sum + part
        dk[span, :] += key_sum.T
        return carry

    lax.fori_loop(begin, end, body, jnp.int32(0))


def own_share(tasks, stage):
    total = tasks[0][3]["own"][1]
    near = tasks[0][3]["near"][1]
    far = tasks[0][3]["far"][1]
    for t in tasks[1:]:
        total = total + t[3]["own"][1]
        near = near + t[3]["near"][1]
        far = far + t[3]["far"][1]
    one = jnp.minimum(total, PRE_CHUNKS)
    two = jnp.minimum(total, one + jnp.maximum(PIECE_CHUNKS - near, 0))
    three = jnp.minimum(total, two + jnp.maximum(PIECE_CHUNKS - far, 0))
    marks = [jnp.int32(0), one, two, three, total]
    return marks[stage], marks[stage + 1], near, far


def regions_of(own_rows):
    return {"far": (0, HALF), "near": (HALF, RIM), "own": (RIM, RIM + own_rows)}


def first_kernel(slot, doc, q, w, nrm, cot, tgt, key, q2, wqt, wb, nm, ct, tg, keys, dq, dk, rb, sems):
    own_rows = key.shape[1]
    copies = [
        pltpu.make_async_copy(key.at[0], keys.at[RIM : RIM + own_rows], sems.at[0]),
        pltpu.make_async_copy(tgt.at[0], tg, sems.at[1]),
    ]
    for copy in copies:
        copy.start()
    tile_rows = w.shape[2]
    heads = w.shape[3]
    depth = q2.shape[2]
    for i in range(w.shape[1]):
        weights = w[0, i] * (1.0 / depth**0.5)
        for h in range(heads):
            here = slice(h * tile_rows, (h + 1) * tile_rows)
            q2[i, here, :] = q[0, i, :, h * depth : (h + 1) * depth]
            wb[i, here, :] = jnp.broadcast_to(weights[:, h : h + 1], (tile_rows, LANES))
        for h in range(0, heads, 2):
            here = slice(h * tile_rows, (h + 2) * tile_rows)
            wide = jnp.concatenate(
                [jnp.broadcast_to(w[0, i, :, u : u + 1], (tile_rows, depth)) for u in (h, h + 1)], axis=0
            )
            wqt[i, :, here] = (q2[i, here, :].astype(f32) * wide).T.astype(bf16)
        nm[i] = jnp.broadcast_to(nrm[0, i : i + 1, :], (LANES, tile_rows)).T
        ct[i] = jnp.broadcast_to(cot[0, i : i + 1, :], (LANES, tile_rows)).T
    dq[...] = jnp.zeros_like(dq)
    dk[...] = jnp.zeros_like(dk)
    for copy in copies:
        copy.wait()
    tasks = task_spans(slot, doc, tile_rows, regions_of(own_rows))
    begin, end, _, _ = own_share(tasks, 0)
    chunk_loop(tasks, "own", begin, end, (q2, wqt, wb, nm, ct, tg, keys, dq, dk, rb))


def piece_kernel(name, slot, doc, rim, q2, wqt, wb, nm, ct, tg, *refs):
    keys, dq, dk, lent, rb = refs[3:]
    tile_rows = nm.shape[1]
    own_rows = keys.shape[0] - RIM
    regions = regions_of(own_rows)
    start, stop = regions[name]
    keys[start:stop, :] = rim[...]
    tasks = task_spans(slot, doc, tile_rows, regions)
    begin, end, near, far = own_share(tasks, 1 if name == "near" else 2)
    st = (q2, wqt, wb, nm, ct, tg, keys, dq, dk, rb)
    chunk_loop(tasks, name, 0, near if name == "near" else far, st)
    lent[...] = (dk[start:stop, :] * UP).astype(bf16)
    chunk_loop(tasks, "own", begin, end, st)


def last_kernel(slot, doc, q2, wqt, wb, nm, ct, tg, keys, dq, dk_in, dk, q_out, w_out, k_out, rb):
    tile_rows = nm.shape[1]
    depth = q2.shape[2]
    own_rows = keys.shape[0] - RIM
    tasks = task_spans(slot, doc, tile_rows, regions_of(own_rows))
    begin, end, _, _ = own_share(tasks, 3)
    chunk_loop(tasks, "own", begin, end, (q2, wqt, wb, nm, ct, tg, keys, dq, dk, rb))
    for i in range(q2.shape[0]):
        for h in range(q2.shape[1] // tile_rows):
            here = slice(h * tile_rows, (h + 1) * tile_rows)
            grad = dq[i, here, :]
            q_out[0, i, :, h * depth : (h + 1) * depth] = (
                grad * (wb[i, here, :] * (UP * depth**0.5))
            ).astype(bf16)
            w_out[0, i, :, h : h + 1] = UP * jnp.sum(
                grad * q2[i, here, :].astype(f32), axis=1, keepdims=True
            )
    k_out[0] = (dk[RIM:, :] * UP).astype(bf16)


def add_kernel(k_in, dk, near, far, k_out, tail, sem):
    own_rows = k_out.shape[1]
    own = dk[RIM + own_rows - RIM :, :] * UP
    tail[:HALF] = (own[:HALF] + far[...].astype(f32)).astype(bf16)
    tail[HALF:] = (own[HALF:] + near[...].astype(f32)).astype(bf16)
    copy = pltpu.make_async_copy(tail, k_out.at[0, own_rows - RIM :], sem)
    copy.start()
    copy.wait()


def local(queries, head_weights, key_vectors, targets, normalizers, loss_grad, tile_slot, doc_start):
    task_count, tile_rows, width = queries.shape[1:]
    heads = head_weights.shape[3]
    own_rows, depth = key_vectors.shape[1:]
    head_rows = heads * tile_rows
    vmem = pl.BlockSpec(memory_space=pltpu.VMEM)
    smem = pl.BlockSpec(memory_space=pltpu.SMEM)
    anywhere = pl.BlockSpec(memory_space=pl.ANY)
    params = pltpu.CompilerParams(vmem_limit_bytes=40 * 2**20)
    hold = lambda shape, kind: pltpu.VMEM(shape, kind)
    keep = lambda x: pltpu.with_memory_space_constraint(x, pltpu.VMEM)

    far_keys = passed_along(key_vectors[0, own_rows - RIM : own_rows - HALF], 1)
    near_keys = passed_along(key_vectors[0, own_rows - HALF :], 1)
    scratch = pltpu.VMEM((head_rows, WIDTH), bf16)
    state = [
        hold((task_count, head_rows, depth), bf16),
        hold((task_count, depth, head_rows), bf16),
        hold((task_count, head_rows, LANES), f32),
        hold((task_count, tile_rows, LANES), f32),
        hold((task_count, tile_rows, LANES), f32),
        hold(targets.shape[1:], bf16),
        hold((RIM + own_rows, depth), bf16),
        hold((task_count, head_rows, depth), f32),
        hold((RIM + own_rows, depth), f32),
    ]
    st = pl.pallas_call(
        first_kernel,
        in_specs=[smem, smem, vmem, vmem, vmem, vmem, anywhere, anywhere],
        out_specs=[vmem] * 9,
        out_shape=state,
        scratch_shapes=[scratch, pltpu.SemaphoreType.DMA((2,))],
        compiler_params=params,
        name="own_first",
    )(tile_slot, doc_start, queries, head_weights, normalizers, loss_grad, targets, key_vectors)
    fixed, moving = st[:6], st[6:]

    def piece(name, rim, moving):
        out = pl.pallas_call(
            functools.partial(piece_kernel, name),
            in_specs=[smem, smem] + [vmem] * 10,
            out_specs=[vmem] * 4,
            out_shape=state[6:] + [hold(rim.shape, bf16)],
            input_output_aliases={9: 0, 10: 1, 11: 2},
            scratch_shapes=[scratch],
            compiler_params=params,
            name="borrowed_" + name,
        )(tile_slot, doc_start, rim, *[keep(x) for x in fixed], *[keep(x) for x in moving])
        return out[:3], out[3]

    moving, near_lent = piece("near", near_keys, moving)
    near_back = passed_along(near_lent, -1)
    moving, far_lent = piece("far", far_keys, moving)
    far_back = passed_along(far_lent, -1)
    dk, q_out, w_out, k_out = pl.pallas_call(
        last_kernel,
        in_specs=[smem, smem] + [vmem] * 9,
        out_specs=[vmem] * 4,
        out_shape=[
            state[8],
            jax.ShapeDtypeStruct(queries.shape, bf16),
            jax.ShapeDtypeStruct(head_weights.shape, f32),
            jax.ShapeDtypeStruct(key_vectors.shape, bf16),
        ],
        input_output_aliases={10: 0},
        scratch_shapes=[scratch],
        compiler_params=params,
        name="own_last",
    )(tile_slot, doc_start, *[keep(x) for x in fixed], *[keep(x) for x in moving])
    k_out = pl.pallas_call(
        add_kernel,
        in_specs=[anywhere, vmem, vmem, vmem],
        out_specs=anywhere,
        out_shape=jax.ShapeDtypeStruct(key_vectors.shape, bf16),
        input_output_aliases={0: 0},
        scratch_shapes=[pltpu.VMEM((RIM, depth), bf16), pltpu.SemaphoreType.DMA],
        compiler_params=params,
        name="add_lent",
    )(k_out, keep(dk), near_back, far_back)
    return q_out, w_out, k_out


def solution(mesh):
    return jax.shard_map(
        local,
        mesh=mesh,
        in_specs=(
            P("sec", "ctx", None, None),
            P("sec", "ctx", None, None),
            P("sec", "ctx", None),
            P("sec", "ctx", None, None),
            P("sec", "ctx", None),
            P("sec", "ctx", None),
            P("sec", "ctx"),
            P("sec", "ctx"),
        ),
        out_specs=(P("sec", "ctx", None, None), P("sec", "ctx", None, None), P("sec", "ctx", None)),
        check_vma=False,
    )
```

```python
import functools

import jax
import jax.numpy as jnp
from jax import lax
from jax.experimental import pallas as pl
from jax.experimental.pallas import tpu as pltpu
from jax.sharding import PartitionSpec as P

BLK = 1024
MAXB = 4
RIM = (MAXB - 1) * BLK
FAR = 1408
WIDTH = 512
LANES = 128
ROWS = 8
PAIR = 16
DOWN = 2.0**-16
UP = 2.0**16
PRE_CHUNKS = 1
NEAR_CHUNKS = 3
FAR_CHUNKS = 3

f32 = jnp.float32
bf16 = jnp.bfloat16


def passed_along(array, by):
    size = lax.axis_size("ctx")
    pairs = [(i, i + by) for i in range(size) if 0 <= i + by < size]
    return lax.ppermute(array, "ctx", pairs)


def segments_of(slot_ref, doc_ref, tile_rows, own_rows, start, stop):
    base = lax.axis_index("ctx") * own_rows - RIM
    out = []
    for i in range(doc_ref.shape[1]):
        doc = doc_ref[0, i] - base
        query = slot_ref[0, i] * tile_rows + RIM
        block = doc // BLK * BLK
        low = jnp.maximum(doc // LANES * LANES, start)
        high = jnp.minimum(query + tile_rows, stop)
        count = jnp.maximum(high - low + WIDTH - 1, 0) // WIDTH
        last = jnp.minimum(RIM + own_rows, block + MAXB * BLK) - WIDTH
        out.append((jnp.int32(i), low, count, last, doc, query, block, jnp.int32(stop)))
    return out


def total_of(segments):
    return sum((s[2] for s in segments[1:]), segments[0][2])


def chunk_loop(segments, skip, end, st):
    q2, wqt, wb, nm, ct, tg, keys, dq, dk, rb, db = st
    head_rows, depth = q2.shape[1:]
    tile_rows = nm.shape[1]
    heads = head_rows // tile_rows
    rows = heads * ROWS
    blocks = tile_rows // ROWS
    factor = DOWN / depth**0.5
    repeat = WIDTH // LANES

    def wide(x):
        return jnp.concatenate([x] * repeat, axis=1)

    def body(step, carry):
        o = jnp.where(step >= skip[0], step + skip[1], step)
        task, low, _, last, doc, query, block, stop = segments[0]
        before = jnp.int32(0)
        seen = jnp.int32(0)
        for i in range(1, len(segments)):
            seen = seen + segments[i - 1][2]
            later = o >= seen
            pick = lambda new, old: jnp.where(later, new, old)
            before = pick(seen, before)
            task = pick(segments[i][0], task)
            low = pick(segments[i][1], low)
            last = pick(segments[i][3], last)
            doc = pick(segments[i][4], doc)
            query = pick(segments[i][5], query)
            block = pick(segments[i][6], block)
            stop = pick(segments[i][7], stop)
        first = low + (o - before) * WIDTH
        start = jnp.clip(jnp.minimum(first, last), 0, keys.shape[0] - WIDTH)
        column = pl.multiple_of(jnp.clip(start - block, 0, tg.shape[2] - WIDTH), LANES)
        start = pl.multiple_of(start, LANES)
        bottom = jnp.maximum(first, doc)
        span = pl.ds(start, WIDTH)
        key = keys[span, :]
        key_row = start + lax.broadcasted_iota(jnp.int32, (ROWS, WIDTH), 1)
        query_row = query + lax.broadcasted_iota(jnp.int32, (ROWS, WIDTH), 0)
        for b in range(blocks):
            here = slice(b * rows, (b + 1) * rows)
            tile = slice(b * ROWS, (b + 1) * ROWS)
            s = lax.dot_general(
                q2[task, here, :], key, (((1,), (1,)), ((), ())), preferred_element_type=f32
            )
            r = jnp.maximum(s, 0.0)
            w = wb[task, here, :]
            index = wide(w[:ROWS]) * r[:ROWS]
            for h in range(1, heads):
                line = slice(h * ROWS, (h + 1) * ROWS)
                index = index + wide(w[line]) * r[line]
            rb[here, :] = r.astype(bf16)
            target = tg[task, tile, pl.ds(column, WIDTH)].astype(f32)
            live = (key_row >= bottom) & (key_row <= jnp.minimum(query_row + b * ROWS, stop - 1))
            delta = wide(ct[task, tile, :]) * (jnp.exp(index - wide(nm[task, tile, :])) - target)
            delta = jnp.where(live, delta * factor, 0.0)
            db[b * PAIR : (b + 1) * PAIR, :] = jnp.concatenate([delta, delta], axis=0).astype(bf16)
        key_sum = None
        for b in range(blocks):
            here = slice(b * rows, (b + 1) * rows)
            delta = jnp.concatenate([db[b * PAIR : (b + 1) * PAIR, :]] * (rows // PAIR), axis=0)
            grad = jnp.where(rb[here, :] > 0, delta, jnp.zeros_like(delta))
            dq[task, here, :] += jnp.dot(grad, key, preferred_element_type=f32)
            part = jnp.dot(wqt[task, :, here], grad, preferred_element_type=f32)
            key_sum = part if key_sum is None else key_sum + part
        dk[span, :] += key_sum.T
        return carry

    lax.fori_loop(0, end, body, jnp.int32(0))


def plan(slot, doc, tile_rows, own_rows):
    spans = {"far": (0, FAR), "near": (FAR, RIM), "own": (RIM, RIM + own_rows)}
    segments = {k: segments_of(slot, doc, tile_rows, own_rows, *v) for k, v in spans.items()}
    near = total_of(segments["near"])
    far = total_of(segments["far"])
    own = total_of(segments["own"])
    one = jnp.minimum(own, PRE_CHUNKS)
    two = jnp.minimum(own, one + jnp.maximum(NEAR_CHUNKS - near, 0))
    three = jnp.minimum(own, two + jnp.maximum(FAR_CHUNKS - far, 0))
    return segments, near, far, (jnp.int32(0), one, two, three, own)


def first_kernel(slot, doc, q, w, nrm, cot, tgt, key, q2, wqt, wb, nm, ct, tg, keys, dq, dk, rb, db, sems):
    own_rows = key.shape[1]
    copies = [
        pltpu.make_async_copy(key.at[0], keys.at[RIM : RIM + own_rows], sems.at[0]),
        pltpu.make_async_copy(tgt.at[0], tg, sems.at[1]),
    ]
    for copy in copies:
        copy.start()
    heads, tile_rows = w.shape[2:]
    depth = q2.shape[2]
    rows = heads * ROWS
    blocks = tile_rows // ROWS
    turn = LANES // ROWS
    for i in range(w.shape[1]):
        plain = w[0, i].T
        nm[i] = jnp.broadcast_to(nrm[0, i : i + 1, :], (LANES, tile_rows)).T
        ct[i] = jnp.broadcast_to(cot[0, i : i + 1, :], (LANES, tile_rows)).T
        for h in range(0, heads, turn):
            queries = [q[0, i, :, u * depth : (u + 1) * depth].astype(f32) for u in range(h, h + turn)]
            weights = [jnp.broadcast_to(plain[:, u : u + 1], (tile_rows, LANES)) for u in range(h, h + turn)]
            for b in range(blocks):
                tile = slice(b * ROWS, (b + 1) * ROWS)
                here = slice(b * rows + h * ROWS, b * rows + (h + turn) * ROWS)
                some = jnp.concatenate([x[tile] for x in queries], axis=0)
                scale = jnp.concatenate([x[tile] for x in weights], axis=0)
                q2[i, here, :] = some.astype(bf16)
                wb[i, here, :] = scale * (1.0 / depth**0.5)
                wqt[i, :, here] = (some * scale).T.astype(bf16)
    dq[...] = jnp.zeros_like(dq)
    dk[...] = jnp.zeros_like(dk)
    for copy in copies:
        copy.wait()
    segments, _, _, marks = plan(slot, doc, tile_rows, own_rows)
    chunk_loop(segments["own"], (marks[1], 0), marks[1], (q2, wqt, wb, nm, ct, tg, keys, dq, dk, rb, db))


def piece_kernel(name, slot, doc, rim, q2, wqt, wb, nm, ct, tg, *refs):
    keys, dq, dk, lent, rb, db = refs[3:]
    tile_rows = nm.shape[1]
    start, stop = (FAR, RIM) if name == "near" else (0, FAR)
    keys[start:stop, :] = rim[...]
    segments, near, far, marks = plan(slot, doc, tile_rows, keys.shape[0] - RIM)
    count, at = (near, 1) if name == "near" else (far, 2)
    st = (q2, wqt, wb, nm, ct, tg, keys, dq, dk, rb, db)
    chunk_loop(segments[name] + segments["own"], (count, marks[at]), count + marks[at + 1] - marks[at], st)
    lent[...] = (dk[start:stop, :] * UP).astype(bf16)


def last_kernel(slot, doc, q2, wqt, wb, nm, ct, tg, keys, dq, dk_in, *refs):
    dk, q_out, w_out, k_out, rb, db, dots, whole, sem = refs
    tile_rows = nm.shape[1]
    head_rows, depth = q2.shape[1:]
    heads = head_rows // tile_rows
    rows = heads * ROWS
    own_rows = keys.shape[0] - RIM
    segments, _, _, marks = plan(slot, doc, tile_rows, own_rows)
    st = (q2, wqt, wb, nm, ct, tg, keys, dq, dk, rb, db)
    chunk_loop(segments["own"], (0, marks[3]), marks[4] - marks[3], st)
    settled = own_rows - RIM
    whole[...] = (dk[RIM : RIM + settled, :] * UP).astype(bf16)
    copy = pltpu.make_async_copy(whole, k_out.at[0, :settled], sem)
    copy.start()
    lane = lax.broadcasted_iota(jnp.int32, (ROWS, LANES), 1)
    for i in range(q2.shape[0]):
        for b in range(0, tile_rows // ROWS, 2):
            sums = [jnp.zeros((ROWS, LANES), f32), jnp.zeros((ROWS, LANES), f32)]
            for h in range(0, heads, 2):
                out = [[], []]
                for c in range(2):
                    at = (b + c) * rows + h * ROWS
                    grad = dq[i, at : at + PAIR, :]
                    dot = grad * q2[i, at : at + PAIR, :].astype(f32)
                    full = grad * (wb[i, at : at + PAIR, :] * (UP * depth**0.5))
                    for u in range(2):
                        line = slice(u * ROWS, (u + 1) * ROWS)
                        out[u].append(full[line])
                        sums[c] = jnp.where(
                            lane == h + u, jnp.sum(dot[line], axis=1, keepdims=True), sums[c]
                        )
                for u in range(2):
                    q_out[0, i, b * ROWS : (b + 2) * ROWS, (h + u) * depth : (h + u + 1) * depth] = (
                        jnp.concatenate(out[u], axis=0).astype(bf16)
                    )
            for c in range(2):
                dots[(b + c) * ROWS : (b + c + 1) * ROWS, :] = sums[c] * UP
        w_out[0, i] = dots[:, :heads].T
    copy.wait()


def add_kernel(k_in, dk, near, far, k_out, tail, sem):
    own_rows = k_out.shape[1]
    own = dk[own_rows:, :] * UP
    tail[:FAR] = (own[:FAR] + far[...].astype(f32)).astype(bf16)
    tail[FAR:] = (own[FAR:] + near[...].astype(f32)).astype(bf16)
    copy = pltpu.make_async_copy(tail, k_out.at[0, own_rows - RIM :], sem)
    copy.start()
    copy.wait()


def local(queries, head_weights, key_vectors, targets, normalizers, loss_grad, tile_slot, doc_start):
    task_count, tile_rows, width = queries.shape[1:]
    heads = head_weights.shape[3]
    own_rows, depth = key_vectors.shape[1:]
    head_rows = heads * tile_rows
    vmem = pl.BlockSpec(memory_space=pltpu.VMEM)
    smem = pl.BlockSpec(memory_space=pltpu.SMEM)
    anywhere = pl.BlockSpec(memory_space=pl.ANY)
    params = pltpu.CompilerParams(vmem_limit_bytes=40 * 2**20)
    heavy = pl.CostEstimate(flops=4 * head_rows * depth * own_rows, bytes_accessed=0, transcendentals=0)
    light = pl.CostEstimate(flops=depth, bytes_accessed=0, transcendentals=0)

    def keep(x):
        return pltpu.with_memory_space_constraint(x, pltpu.VMEM)

    near_keys = passed_along(key_vectors[0, own_rows - RIM + FAR :], 1)
    far_keys = passed_along(key_vectors[0, own_rows - RIM : own_rows - RIM + FAR], 1)
    scratch = [pltpu.VMEM((head_rows, WIDTH), bf16), pltpu.VMEM((tile_rows * PAIR // ROWS, WIDTH), bf16)]
    state = [
        pltpu.VMEM((task_count, head_rows, depth), bf16),
        pltpu.VMEM((task_count, depth, head_rows), bf16),
        pltpu.VMEM((task_count, head_rows, LANES), f32),
        pltpu.VMEM((task_count, tile_rows, LANES), f32),
        pltpu.VMEM((task_count, tile_rows, LANES), f32),
        pltpu.VMEM(targets.shape[1:], bf16),
        pltpu.VMEM((RIM + own_rows, depth), bf16),
        pltpu.VMEM((task_count, head_rows, depth), f32),
        pltpu.VMEM((RIM + own_rows, depth), f32),
    ]
    flipped = jnp.swapaxes(head_weights, 2, 3)
    st = pl.pallas_call(
        first_kernel,
        in_specs=[smem, smem, vmem, vmem, vmem, vmem, anywhere, anywhere],
        out_specs=[vmem] * 9,
        out_shape=state,
        scratch_shapes=scratch + [pltpu.SemaphoreType.DMA((2,))],
        compiler_params=params,
        cost_estimate=heavy,
        name="own_first",
    )(tile_slot, doc_start, queries, flipped, normalizers, loss_grad, targets, key_vectors)
    fixed, moving = st[:6], st[6:]

    def piece(name, rim, moving):
        out = pl.pallas_call(
            functools.partial(piece_kernel, name),
            in_specs=[smem, smem] + [vmem] * 10,
            out_specs=[vmem] * 4,
            out_shape=state[6:] + [pltpu.VMEM(rim.shape, bf16)],
            input_output_aliases={9: 0, 10: 1, 11: 2},
            scratch_shapes=scratch,
            compiler_params=params,
            cost_estimate=heavy,
            name="borrowed_" + name,
        )(tile_slot, doc_start, keep(rim), *[keep(x) for x in fixed], *[keep(x) for x in moving])
        return out[:3], out[3]

    moving, near_lent = piece("near", near_keys, moving)
    near_back = passed_along(near_lent, -1)
    moving, far_lent = piece("far", far_keys, moving)
    far_back = passed_along(far_lent, -1)
    dk, q_out, w_out, k_out = pl.pallas_call(
        last_kernel,
        in_specs=[smem, smem] + [vmem] * 9,
        out_specs=[vmem] * 3 + [anywhere],
        out_shape=[
            state[8],
            jax.ShapeDtypeStruct(queries.shape, bf16),
            jax.ShapeDtypeStruct(flipped.shape, f32),
            pltpu.HBM(key_vectors.shape, bf16),
        ],
        input_output_aliases={10: 0},
        scratch_shapes=scratch
        + [
            pltpu.VMEM((tile_rows, LANES), f32),
            pltpu.VMEM((own_rows - RIM, depth), bf16),
            pltpu.SemaphoreType.DMA,
        ],
        compiler_params=params,
        cost_estimate=light,
        name="own_last",
    )(tile_slot, doc_start, *[keep(x) for x in fixed], *[keep(x) for x in moving])
    k_out = pl.pallas_call(
        add_kernel,
        in_specs=[anywhere, vmem, vmem, vmem],
        out_specs=anywhere,
        out_shape=pltpu.HBM(key_vectors.shape, bf16),
        input_output_aliases={0: 0},
        scratch_shapes=[pltpu.VMEM((RIM, depth), bf16), pltpu.SemaphoreType.DMA],
        compiler_params=params,
        name="add_lent",
    )(k_out, keep(dk), keep(near_back), keep(far_back))
    return q_out, jnp.swapaxes(w_out, 2, 3), k_out


def solution(mesh):
    return jax.shard_map(
        local,
        mesh=mesh,
        in_specs=(
            P("sec", "ctx", None, None),
            P("sec", "ctx", None, None),
            P("sec", "ctx", None),
            P("sec", "ctx", None, None),
            P("sec", "ctx", None),
            P("sec", "ctx", None),
            P("sec", "ctx"),
            P("sec", "ctx"),
        ),
        out_specs=(P("sec", "ctx", None, None), P("sec", "ctx", None, None), P("sec", "ctx", None)),
        check_vma=False,
    )
```

```python
import functools

import jax
import jax.numpy as jnp
from jax import lax
from jax.experimental import pallas as pl
from jax.experimental.pallas import tpu as pltpu
from jax.sharding import PartitionSpec as P

BLK = 1024
MAXB = 4
RIM = (MAXB - 1) * BLK
FAR = RIM // 2
EXTRA = 16
WIDTH = 512
LANES = 128
ROWS = 8
PAIR = 16
DOWN = 2.0**-16
UP = 2.0**16
PRE_CHUNKS = 2
NEAR_CHUNKS = 4
FAR_CHUNKS = 4

f32 = jnp.float32
bf16 = jnp.bfloat16


def passed_along(array, by):
    size = lax.axis_size("ctx")
    pairs = [(i, i + by) for i in range(size) if 0 <= i + by < size]
    return lax.ppermute(array, "ctx", pairs)


def segments_of(slot_ref, doc_ref, tile_rows, own_rows):
    base = lax.axis_index("ctx") * own_rows - RIM
    out = {"far": [], "near": [], "own": []}

    def chunks(low, high):
        return jnp.maximum(high - low + WIDTH - 1, 0) // WIDTH

    for i in range(doc_ref.shape[1]):
        doc = doc_ref[0, i] - base
        query = slot_ref[0, i] * tile_rows + RIM
        block = doc // BLK * BLK
        last = jnp.minimum(RIM + own_rows, block + MAXB * BLK) - WIDTH
        end = query + tile_rows
        low = doc // LANES * LANES
        near_low = jnp.maximum(low, FAR)
        count = {"far": chunks(low, FAR), "near": chunks(near_low, RIM)}
        own_low = near_low + count["near"] * WIDTH
        count["own"] = chunks(own_low, end)
        lows = {"far": low, "near": near_low, "own": own_low}
        for name in out:
            stop = jnp.int32(FAR) if name == "far" else end
            out[name].append((jnp.int32(i), lows[name], count[name], last, doc, query, block, stop))
    return out


def total_of(segments):
    return sum((s[2] for s in segments[1:]), segments[0][2])


def chunk_loop(segments, skip, end, st):
    q2, wqt, wb, nm, ct, tg, keys, dq, dk, rb, db = st
    head_rows, depth = q2.shape[1:]
    tile_rows = nm.shape[1]
    heads = head_rows // tile_rows
    rows = heads * ROWS
    blocks = tile_rows // ROWS
    factor = DOWN / depth**0.5
    repeat = WIDTH // LANES

    def wide(x):
        return jnp.concatenate([x] * repeat, axis=1)

    def locate(step):
        o = jnp.where(step >= skip[0], step + skip[1], step)
        task, low, _, last, doc, query, block, stop = segments[0]
        before = jnp.int32(0)
        seen = jnp.int32(0)
        for i in range(1, len(segments)):
            seen = seen + segments[i - 1][2]
            later = o >= seen
            pick = lambda new, old: jnp.where(later, new, old)
            before = pick(seen, before)
            task = pick(segments[i][0], task)
            low = pick(segments[i][1], low)
            last = pick(segments[i][3], last)
            doc = pick(segments[i][4], doc)
            query = pick(segments[i][5], query)
            block = pick(segments[i][6], block)
            stop = pick(segments[i][7], stop)
        first = low + (o - before) * WIDTH
        start = jnp.clip(jnp.minimum(first, last), 0, keys.shape[0] - WIDTH)
        column = jnp.clip(start - block, 0, tg.shape[2] - WIDTH)
        return task, start, column, jnp.maximum(first, doc), query, stop

    def load(at):
        span = pl.ds(pl.multiple_of(at[1], LANES), WIDTH)
        return span, keys[span, :]

    def scores(b, at, key):
        task, start, column, bottom, query, stop = at
        here = slice(b * rows, (b + 1) * rows)
        tile = slice(b * ROWS, (b + 1) * ROWS)
        s = lax.dot_general(
            q2[task, here, :], key, (((1,), (1,)), ((), ())), preferred_element_type=f32
        )
        r = jnp.maximum(s, 0.0)
        w = wb[task, here, :]
        index = wide(w[:ROWS]) * r[:ROWS]
        for h in range(1, heads):
            line = slice(h * ROWS, (h + 1) * ROWS)
            index = index + wide(w[line]) * r[line]
        rb[here, :] = r.astype(bf16)
        target = tg[task, tile, pl.ds(pl.multiple_of(column, LANES), WIDTH)].astype(f32)
        key_row = start + lax.broadcasted_iota(jnp.int32, (ROWS, WIDTH), 1)
        query_row = query + b * ROWS + lax.broadcasted_iota(jnp.int32, (ROWS, WIDTH), 0)
        live = (key_row >= bottom) & (key_row <= jnp.minimum(query_row, stop - 1))
        delta = wide(ct[task, tile, :]) * (jnp.exp(index - wide(nm[task, tile, :])) - target)
        delta = jnp.where(live, delta * factor, 0.0)
        db[b * PAIR : (b + 1) * PAIR, :] = jnp.concatenate([delta, delta], axis=0).astype(bf16)

    def grads(b, at, key, key_sum):
        here = slice(b * rows, (b + 1) * rows)
        delta = jnp.concatenate([db[b * PAIR : (b + 1) * PAIR, :]] * (rows // PAIR), axis=0)
        grad = jnp.where(rb[here, :] > 0, delta, jnp.zeros_like(delta))
        dq[at[0], here, :] += jnp.dot(grad, key, preferred_element_type=f32)
        part = jnp.dot(wqt[at[0], :, here], grad, preferred_element_type=f32)
        return part if key_sum is None else key_sum + part

    @pl.when(end > 0)
    def _():
        at = locate(jnp.int32(0))
        _, key = load(at)
        for b in range(blocks):
            scores(b, at, key)

        def body(step, old):
            at = locate(step)
            span, old_key = load(old)
            _, key = load(at)
            key_sum = None
            for b in range(blocks):
                key_sum = grads(b, old, old_key, key_sum)
                scores(b, at, key)
            dk[span, :] += key_sum.T
            return at

        at = lax.fori_loop(1, end, body, at)
        span, key = load(at)
        key_sum = None
        for b in range(blocks):
            key_sum = grads(b, at, key, key_sum)
        dk[span, :] += key_sum.T


def plan(slot, doc, tile_rows, own_rows):
    segments = segments_of(slot, doc, tile_rows, own_rows)
    near = total_of(segments["near"])
    far = total_of(segments["far"])
    own = total_of(segments["own"])
    one = jnp.minimum(own, PRE_CHUNKS)
    two = jnp.minimum(own, one + jnp.maximum(NEAR_CHUNKS - near, 0))
    three = jnp.minimum(own, two + jnp.maximum(FAR_CHUNKS - far, 0))
    return segments, near, far, (jnp.int32(0), one, two, three, own)


def first_kernel(slot, doc, q, w, nrm, cot, tgt, key, q2, wqt, wb, nm, ct, tg, keys, dq, dk, far, rb, db, q_in, sems):
    own_rows = key.shape[1]
    copies = [
        pltpu.make_async_copy(q.at[0], q_in, sems.at[0]),
        pltpu.make_async_copy(key.at[0], keys.at[RIM : RIM + own_rows], sems.at[1]),
        pltpu.make_async_copy(tgt.at[0], tg, sems.at[2]),
    ]
    for copy in copies:
        copy.start()
    dq[...] = jnp.zeros_like(dq)
    dk[...] = jnp.zeros_like(dk)
    copies[0].wait()
    heads, tile_rows = w.shape[2:]
    depth = q2.shape[2]
    rows = heads * ROWS
    blocks = tile_rows // ROWS
    turn = LANES // ROWS
    for i in range(w.shape[1]):
        plain = w[0, i].T
        nm[i] = jnp.broadcast_to(nrm[0, i : i + 1, :], (LANES, tile_rows)).T
        ct[i] = jnp.broadcast_to(cot[0, i : i + 1, :], (LANES, tile_rows)).T
        for h in range(0, heads, turn):
            queries = [q_in[i, :, u * depth : (u + 1) * depth].astype(f32) for u in range(h, h + turn)]
            weights = [jnp.broadcast_to(plain[:, u : u + 1], (tile_rows, LANES)) for u in range(h, h + turn)]
            for b in range(blocks):
                tile = slice(b * ROWS, (b + 1) * ROWS)
                here = slice(b * rows + h * ROWS, b * rows + (h + turn) * ROWS)
                some = jnp.concatenate([x[tile] for x in queries], axis=0)
                scale = jnp.concatenate([x[tile] for x in weights], axis=0)
                q2[i, here, :] = some.astype(bf16)
                wb[i, here, :] = scale * (1.0 / depth**0.5)
                wqt[i, :, here] = (some * scale).T.astype(bf16)
    copies[1].wait()
    copies[2].wait()
    far[...] = keys[own_rows : own_rows + FAR, :]
    segments, _, _, marks = plan(slot, doc, tile_rows, own_rows)
    chunk_loop(segments["own"], (marks[1], 0), marks[1], (q2, wqt, wb, nm, ct, tg, keys, dq, dk, rb, db))


def piece_kernel(name, slot, doc, rim, q2, wqt, wb, nm, ct, tg, *refs):
    keys, dq, dk, lent, rb, db = refs[3:]
    tile_rows = nm.shape[1]
    start, stop = (FAR, RIM) if name == "near" else (0, FAR)
    keys[start:stop, :] = rim[...]
    segments, near, far, marks = plan(slot, doc, tile_rows, keys.shape[0] - RIM)
    count, at = (near, 1) if name == "near" else (far, 2)
    st = (q2, wqt, wb, nm, ct, tg, keys, dq, dk, rb, db)
    chunk_loop(segments[name] + segments["own"], (count, marks[at]), count + marks[at + 1] - marks[at], st)
    lent[: stop - start, :] = (dk[start:stop, :] * UP).astype(bf16)
    if name == "near":
        lent[stop - start :, :] = jnp.zeros((EXTRA, lent.shape[1]), bf16)


def last_kernel(slot, doc, q2, wqt, wb, nm, ct, tg, keys, dq, dk_in, *refs):
    dk, q_out, w_out, k_out, rb, db, dots, whole, full_q, sems = refs
    tile_rows = nm.shape[1]
    head_rows, depth = q2.shape[1:]
    heads = head_rows // tile_rows
    rows = heads * ROWS
    own_rows = keys.shape[0] - RIM
    segments, _, _, marks = plan(slot, doc, tile_rows, own_rows)
    st = (q2, wqt, wb, nm, ct, tg, keys, dq, dk, rb, db)
    chunk_loop(segments["own"], (0, marks[3]), marks[4] - marks[3], st)
    copies = []
    for i in range(q2.shape[0]):
        for b in range(0, tile_rows // ROWS, 2):
            for h in range(0, heads, 2):
                full = []
                for c in range(2):
                    at = (b + c) * rows + h * ROWS
                    full.append(dq[i, at : at + PAIR, :] * (wb[i, at : at + PAIR, :] * (UP * depth**0.5)))
                for u in range(2):
                    line = slice(u * ROWS, (u + 1) * ROWS)
                    full_q[i, b * ROWS : (b + 2) * ROWS, (h + u) * depth : (h + u + 1) * depth] = (
                        jnp.concatenate([full[0][line], full[1][line]], axis=0).astype(bf16)
                    )
        copies.append(pltpu.make_async_copy(full_q.at[i], q_out.at[0, i], sems.at[i]))
        copies[-1].start()
    settled = own_rows - RIM
    whole[...] = (dk[RIM : RIM + settled, :] * UP).astype(bf16)
    copies.append(pltpu.make_async_copy(whole, k_out.at[0, :settled], sems.at[q2.shape[0]]))
    copies[-1].start()
    lane = lax.broadcasted_iota(jnp.int32, (ROWS, LANES), 1)
    for i in range(q2.shape[0]):
        for b in range(tile_rows // ROWS):
            sums = jnp.zeros((ROWS, LANES), f32)
            for h in range(0, heads, 2):
                at = slice(b * rows + h * ROWS, b * rows + h * ROWS + PAIR)
                dot = dq[i, at, :] * q2[i, at, :].astype(f32)
                for u in range(2):
                    line = slice(u * ROWS, (u + 1) * ROWS)
                    sums = jnp.where(lane == h + u, jnp.sum(dot[line], axis=1, keepdims=True), sums)
            dots[b * ROWS : (b + 1) * ROWS, :] = sums * UP
        w_out[0, i] = dots[:, :heads].T
    for copy in copies:
        copy.wait()


def add_kernel(k_in, dk, near, far, k_out, tail, sem):
    own_rows = k_out.shape[1]
    own = dk[own_rows:, :] * UP
    tail[:FAR] = (own[:FAR] + far[...].astype(f32)).astype(bf16)
    tail[FAR:] = (own[FAR:] + near[: RIM - FAR].astype(f32)).astype(bf16)
    copy = pltpu.make_async_copy(tail, k_out.at[0, own_rows - RIM :], sem)
    copy.start()
    copy.wait()


def local(queries, head_weights, key_vectors, targets, normalizers, loss_grad, tile_slot, doc_start):
    task_count, tile_rows, width = queries.shape[1:]
    heads = head_weights.shape[3]
    own_rows, depth = key_vectors.shape[1:]
    head_rows = heads * tile_rows
    vmem = pl.BlockSpec(memory_space=pltpu.VMEM)
    smem = pl.BlockSpec(memory_space=pltpu.SMEM)
    anywhere = pl.BlockSpec(memory_space=pl.ANY)
    params = pltpu.CompilerParams(vmem_limit_bytes=40 * 2**20)
    heavy = pl.CostEstimate(flops=4 * head_rows * depth * own_rows, bytes_accessed=0, transcendentals=0)
    light = pl.CostEstimate(flops=depth, bytes_accessed=0, transcendentals=0)

    def keep(x):
        return pltpu.with_memory_space_constraint(x, pltpu.VMEM)

    near_keys = passed_along(key_vectors[0, own_rows - RIM + FAR :], 1)
    scratch = [pltpu.VMEM((head_rows, WIDTH), bf16), pltpu.VMEM((tile_rows * PAIR // ROWS, WIDTH), bf16)]
    state = [
        pltpu.VMEM((task_count, head_rows, depth), bf16),
        pltpu.VMEM((task_count, depth, head_rows), bf16),
        pltpu.VMEM((task_count, head_rows, LANES), f32),
        pltpu.VMEM((task_count, tile_rows, LANES), f32),
        pltpu.VMEM((task_count, tile_rows, LANES), f32),
        pltpu.VMEM(targets.shape[1:], bf16),
        pltpu.VMEM((RIM + own_rows, depth), bf16),
        pltpu.VMEM((task_count, head_rows, depth), f32),
        pltpu.VMEM((RIM + own_rows, depth), f32),
    ]
    flipped = jnp.swapaxes(head_weights, 2, 3)
    st = pl.pallas_call(
        first_kernel,
        in_specs=[smem, smem, anywhere, vmem, vmem, vmem, anywhere, anywhere],
        out_specs=[vmem] * 10,
        out_shape=state + [pltpu.VMEM((FAR, depth), bf16)],
        scratch_shapes=scratch + [pltpu.VMEM(queries.shape[1:], bf16), pltpu.SemaphoreType.DMA((3,))],
        compiler_params=params,
        cost_estimate=heavy,
        name="own_first",
    )(tile_slot, doc_start, queries, flipped, normalizers, loss_grad, targets, key_vectors)
    fixed, moving = st[:6], st[6:9]
    far_keys = passed_along(keep(st[9]), 1)

    def piece(name, rim, moving):
        out = pl.pallas_call(
            functools.partial(piece_kernel, name),
            in_specs=[smem, smem] + [vmem] * 10,
            out_specs=[vmem] * 4,
            out_shape=state[6:] + [pltpu.VMEM((rim.shape[0] + (EXTRA if name == "near" else 0), depth), bf16)],
            input_output_aliases={9: 0, 10: 1, 11: 2},
            scratch_shapes=scratch,
            compiler_params=params,
            cost_estimate=heavy,
            name="borrowed_" + name,
        )(tile_slot, doc_start, keep(rim), *[keep(x) for x in fixed], *[keep(x) for x in moving])
        return out[:3], out[3]

    moving, near_lent = piece("near", near_keys, moving)
    near_back = passed_along(near_lent, -1)
    moving, far_lent = piece("far", far_keys, moving)
    far_back = passed_along(far_lent, -1)
    dk, q_out, w_out, k_out = pl.pallas_call(
        last_kernel,
        in_specs=[smem, smem] + [vmem] * 9,
        out_specs=[vmem, anywhere, vmem, anywhere],
        out_shape=[
            state[8],
            pltpu.HBM(queries.shape, bf16),
            jax.ShapeDtypeStruct(flipped.shape, f32),
            pltpu.HBM(key_vectors.shape, bf16),
        ],
        input_output_aliases={10: 0},
        scratch_shapes=scratch
        + [
            pltpu.VMEM((tile_rows, LANES), f32),
            pltpu.VMEM((own_rows - RIM, depth), bf16),
            pltpu.VMEM(queries.shape[1:], bf16),
            pltpu.SemaphoreType.DMA((1 + task_count,)),
        ],
        compiler_params=params,
        cost_estimate=light,
        name="own_last",
    )(tile_slot, doc_start, *[keep(x) for x in fixed], *[keep(x) for x in moving])
    k_out = pl.pallas_call(
        add_kernel,
        in_specs=[anywhere, vmem, vmem, vmem],
        out_specs=anywhere,
        out_shape=pltpu.HBM(key_vectors.shape, bf16),
        input_output_aliases={0: 0},
        scratch_shapes=[pltpu.VMEM((RIM, depth), bf16), pltpu.SemaphoreType.DMA],
        compiler_params=params,
        name="add_lent",
    )(k_out, keep(dk), keep(near_back), keep(far_back))
    return q_out, jnp.swapaxes(w_out, 2, 3), k_out


def solution(mesh):
    return jax.shard_map(
        local,
        mesh=mesh,
        in_specs=(
            P("sec", "ctx", None, None),
            P("sec", "ctx", None, None),
            P("sec", "ctx", None),
            P("sec", "ctx", None, None),
            P("sec", "ctx", None),
            P("sec", "ctx", None),
            P("sec", "ctx"),
            P("sec", "ctx"),
        ),
        out_specs=(P("sec", "ctx", None, None), P("sec", "ctx", None, None), P("sec", "ctx", None)),
        check_vma=False,
    )
```

```python
import functools

import jax
import jax.numpy as jnp
from jax import lax
from jax.experimental import pallas as pl
from jax.experimental.pallas import tpu as pltpu
from jax.sharding import PartitionSpec as P

BLK = 1024
MAXB = 4
RIM = (MAXB - 1) * BLK
FAR = RIM // 2
EXTRA = 16
WIDTH = 512
LANES = 128
ROWS = 8
PAIR = 16
DOWN = 2.0**-16
UP = 2.0**16
PRE_CHUNKS = 2
NEAR_CHUNKS = 5
FAR_CHUNKS = 3

f32 = jnp.float32
bf16 = jnp.bfloat16


def passed_along(array, by):
    size = lax.axis_size("ctx")
    pairs = [(i, i + by) for i in range(size) if 0 <= i + by < size]
    return lax.ppermute(array, "ctx", pairs)


def segments_of(slot_ref, doc_ref, tile_rows, own_rows):
    base = lax.axis_index("ctx") * own_rows - RIM
    out = {"far": [], "near": [], "own": []}

    def chunks(low, high):
        return jnp.maximum(high - low + WIDTH - 1, 0) // WIDTH

    for i in range(doc_ref.shape[1]):
        doc = doc_ref[0, i] - base
        query = slot_ref[0, i] * tile_rows + RIM
        block = doc // BLK * BLK
        last = jnp.minimum(RIM + own_rows, block + MAXB * BLK) - WIDTH
        end = query + tile_rows
        low = doc // LANES * LANES
        near_low = jnp.maximum(low, FAR)
        count = {"far": chunks(low, FAR), "near": chunks(near_low, RIM)}
        own_low = near_low + count["near"] * WIDTH
        count["own"] = chunks(own_low, end)
        lows = {"far": low, "near": near_low, "own": own_low}
        for name in out:
            stop = jnp.int32(FAR) if name == "far" else end
            out[name].append((jnp.int32(i), lows[name], count[name], last, doc, query, block, stop))
    return out


def total_of(segments):
    return sum((s[2] for s in segments[1:]), segments[0][2])


def chunk_loop(segments, skip, end, st):
    q2, wqt, wb, nm, ct, tg, keys, dq, dk, rb, db = st
    head_rows, depth = q2.shape[1:]
    tile_rows = nm.shape[1]
    heads = head_rows // tile_rows
    rows = heads * ROWS
    blocks = tile_rows // ROWS
    factor = DOWN / depth**0.5
    repeat = WIDTH // LANES

    def wide(x):
        return jnp.concatenate([x] * repeat, axis=1)

    def locate(step):
        o = jnp.where(step >= skip[0], step + skip[1], step)
        task, low, _, last, doc, query, block, stop = segments[0]
        before = jnp.int32(0)
        seen = jnp.int32(0)
        for i in range(1, len(segments)):
            seen = seen + segments[i - 1][2]
            later = o >= seen
            pick = lambda new, old: jnp.where(later, new, old)
            before = pick(seen, before)
            task = pick(segments[i][0], task)
            low = pick(segments[i][1], low)
            last = pick(segments[i][3], last)
            doc = pick(segments[i][4], doc)
            query = pick(segments[i][5], query)
            block = pick(segments[i][6], block)
            stop = pick(segments[i][7], stop)
        first = low + (o - before) * WIDTH
        start = jnp.clip(jnp.minimum(first, last), 0, keys.shape[0] - WIDTH)
        column = jnp.clip(start - block, 0, tg.shape[2] - WIDTH)
        return task, start, column, jnp.maximum(first, doc), query, stop

    def load(at):
        span = pl.ds(pl.multiple_of(at[1], LANES), WIDTH)
        return span, keys[span, :]

    def scores(b, at, key):
        task, start, column, bottom, query, stop = at
        here = slice(b * rows, (b + 1) * rows)
        tile = slice(b * ROWS, (b + 1) * ROWS)
        s = lax.dot_general(
            q2[task, here, :], key, (((1,), (1,)), ((), ())), preferred_element_type=f32
        )
        r = jnp.maximum(s, 0.0)
        w = wb[task, here, :]
        index = wide(w[:ROWS]) * r[:ROWS]
        for h in range(1, heads):
            line = slice(h * ROWS, (h + 1) * ROWS)
            index = index + wide(w[line]) * r[line]
        rb[here, :] = r.astype(bf16)
        target = tg[task, tile, pl.ds(pl.multiple_of(column, LANES), WIDTH)].astype(f32)
        key_row = start + lax.broadcasted_iota(jnp.int32, (ROWS, WIDTH), 1)
        query_row = query + b * ROWS + lax.broadcasted_iota(jnp.int32, (ROWS, WIDTH), 0)
        live = (key_row >= bottom) & (key_row <= jnp.minimum(query_row, stop - 1))
        delta = wide(ct[task, tile, :]) * (jnp.exp(index - wide(nm[task, tile, :])) - target)
        delta = jnp.where(live, delta * factor, 0.0)
        db[b * PAIR : (b + 1) * PAIR, :] = jnp.concatenate([delta, delta], axis=0).astype(bf16)

    def grads(b, at, key, key_sum):
        here = slice(b * rows, (b + 1) * rows)
        delta = jnp.concatenate([db[b * PAIR : (b + 1) * PAIR, :]] * (rows // PAIR), axis=0)
        grad = jnp.where(rb[here, :] > 0, delta, jnp.zeros_like(delta))
        part = jnp.dot(wqt[at[0], :, here], grad, preferred_element_type=f32)
        key_sum = part if key_sum is None else key_sum + part
        dq[at[0], here, :] += jnp.dot(grad, key, preferred_element_type=f32)
        return key_sum

    @pl.when(end > 0)
    def _():
        at = locate(jnp.int32(0))
        _, key = load(at)
        for b in range(blocks):
            scores(b, at, key)

        def body(step, old):
            at = locate(step)
            span, old_key = load(old)
            _, key = load(at)
            key_sum = None
            for b in range(blocks):
                key_sum = grads(b, old, old_key, key_sum)
                scores(b, at, key)
            dk[span, :] += key_sum.T
            return at

        at = lax.fori_loop(1, end, body, at)
        span, key = load(at)
        key_sum = None
        for b in range(blocks):
            key_sum = grads(b, at, key, key_sum)
        dk[span, :] += key_sum.T


def plan(slot, doc, tile_rows, own_rows):
    segments = segments_of(slot, doc, tile_rows, own_rows)
    near = total_of(segments["near"])
    far = total_of(segments["far"])
    own = total_of(segments["own"])
    one = jnp.minimum(own, PRE_CHUNKS)
    two = jnp.minimum(own, one + jnp.maximum(NEAR_CHUNKS - near, 0))
    three = jnp.minimum(own, two + jnp.maximum(FAR_CHUNKS - far, 0))
    return segments, near, far, (jnp.int32(0), one, two, three, own)


def first_kernel(slot, doc, q, w, nrm, cot, tgt, key, q2, wqt, wb, nm, ct, tg, keys, dq, dk, far, rb, db, q_in, sems):
    own_rows = key.shape[1]
    copies = [
        pltpu.make_async_copy(q.at[0], q_in, sems.at[0]),
        pltpu.make_async_copy(key.at[0], keys.at[RIM : RIM + own_rows], sems.at[1]),
        pltpu.make_async_copy(tgt.at[0], tg, sems.at[2]),
    ]
    for copy in copies:
        copy.start()
    heads, tile_rows = w.shape[2:]
    depth = q2.shape[2]
    rows = heads * ROWS
    blocks = tile_rows // ROWS
    turn = LANES // ROWS
    dq[...] = jnp.zeros_like(dq)
    dk[...] = jnp.zeros_like(dk)
    for i in range(w.shape[1]):
        plain = w[0, i].T * (1.0 / depth**0.5)
        nm[i] = jnp.broadcast_to(nrm[0, i : i + 1, :], (LANES, tile_rows)).T
        ct[i] = jnp.broadcast_to(cot[0, i : i + 1, :], (LANES, tile_rows)).T
        for h in range(heads):
            column = jnp.broadcast_to(plain[:, h : h + 1], (tile_rows, LANES))
            for b in range(blocks):
                wb[i, b * rows + h * ROWS : b * rows + (h + 1) * ROWS, :] = column[b * ROWS : (b + 1) * ROWS]
    copies[0].wait()
    for i in range(w.shape[1]):
        for h in range(0, heads, turn):
            queries = [q_in[i, :, u * depth : (u + 1) * depth].astype(f32) for u in range(h, h + turn)]
            for b in range(blocks):
                here = slice(b * rows + h * ROWS, b * rows + (h + turn) * ROWS)
                some = jnp.concatenate([x[b * ROWS : (b + 1) * ROWS] for x in queries], axis=0)
                q2[i, here, :] = some.astype(bf16)
                wqt[i, :, here] = (some * wb[i, here, :]).astype(bf16).T
    copies[1].wait()
    copies[2].wait()
    far[...] = keys[own_rows : own_rows + FAR, :]
    segments, _, _, marks = plan(slot, doc, tile_rows, own_rows)
    chunk_loop(segments["own"], (marks[1], 0), marks[1], (q2, wqt, wb, nm, ct, tg, keys, dq, dk, rb, db))


def piece_kernel(name, slot, doc, rim, q2, wqt, wb, nm, ct, tg, *refs):
    keys, dq, dk, lent, rb, db = refs[3:]
    tile_rows = nm.shape[1]
    start, stop = (FAR, RIM) if name == "near" else (0, FAR)
    keys[start:stop, :] = rim[...]
    segments, near, far, marks = plan(slot, doc, tile_rows, keys.shape[0] - RIM)
    count, at = (near, 1) if name == "near" else (far, 2)
    st = (q2, wqt, wb, nm, ct, tg, keys, dq, dk, rb, db)
    chunk_loop(segments[name] + segments["own"], (count, marks[at]), count + marks[at + 1] - marks[at], st)
    lent[: stop - start, :] = (dk[start:stop, :] * (UP * q2.shape[2] ** 0.5)).astype(bf16)
    if name == "near":
        lent[stop - start :, :] = jnp.zeros((EXTRA, lent.shape[1]), bf16)


def last_kernel(slot, doc, q2, wqt, wb, nm, ct, tg, keys, dq, dk_in, *refs):
    dk, q_out, w_out, k_out, rb, db, dots, whole, full_q, sems = refs
    tile_rows = nm.shape[1]
    head_rows, depth = q2.shape[1:]
    heads = head_rows // tile_rows
    rows = heads * ROWS
    own_rows = keys.shape[0] - RIM
    segments, _, _, marks = plan(slot, doc, tile_rows, own_rows)
    st = (q2, wqt, wb, nm, ct, tg, keys, dq, dk, rb, db)
    chunk_loop(segments["own"], (0, marks[3]), marks[4] - marks[3], st)
    copies = []
    for i in range(q2.shape[0]):
        for b in range(0, tile_rows // ROWS, 2):
            for h in range(0, heads, 2):
                full = []
                for c in range(2):
                    at = (b + c) * rows + h * ROWS
                    full.append(dq[i, at : at + PAIR, :] * (wb[i, at : at + PAIR, :] * (UP * depth**0.5)))
                for u in range(2):
                    line = slice(u * ROWS, (u + 1) * ROWS)
                    full_q[i, b * ROWS : (b + 2) * ROWS, (h + u) * depth : (h + u + 1) * depth] = (
                        jnp.concatenate([full[0][line], full[1][line]], axis=0).astype(bf16)
                    )
        copies.append(pltpu.make_async_copy(full_q.at[i], q_out.at[0, i], sems.at[i]))
        copies[-1].start()
    settled = own_rows - RIM
    whole[...] = (dk[RIM : RIM + settled, :] * (UP * depth**0.5)).astype(bf16)
    copies.append(pltpu.make_async_copy(whole, k_out.at[0, :settled], sems.at[q2.shape[0]]))
    copies[-1].start()
    lane = lax.broadcasted_iota(jnp.int32, (ROWS, LANES), 1)
    for i in range(q2.shape[0]):
        for b in range(tile_rows // ROWS):
            sums = jnp.zeros((ROWS, LANES), f32)
            for h in range(0, heads, 2):
                at = slice(b * rows + h * ROWS, b * rows + h * ROWS + PAIR)
                dot = dq[i, at, :] * q2[i, at, :].astype(f32)
                for u in range(2):
                    line = slice(u * ROWS, (u + 1) * ROWS)
                    sums = jnp.where(lane == h + u, jnp.sum(dot[line], axis=1, keepdims=True), sums)
            dots[b * ROWS : (b + 1) * ROWS, :] = sums * UP
        w_out[0, i] = dots[:, :heads].T
    for copy in copies:
        copy.wait()


def add_kernel(k_in, dk, near, far, k_out, tail, sem):
    own_rows = k_out.shape[1]
    own = dk[own_rows:, :] * (UP * dk.shape[1] ** 0.5)
    tail[:FAR] = (own[:FAR] + far[...].astype(f32)).astype(bf16)
    tail[FAR:] = (own[FAR:] + near[: RIM - FAR].astype(f32)).astype(bf16)
    copy = pltpu.make_async_copy(tail, k_out.at[0, own_rows - RIM :], sem)
    copy.start()
    copy.wait()


def local(queries, head_weights, key_vectors, targets, normalizers, loss_grad, tile_slot, doc_start):
    task_count, tile_rows, width = queries.shape[1:]
    heads = head_weights.shape[3]
    own_rows, depth = key_vectors.shape[1:]
    head_rows = heads * tile_rows
    vmem = pl.BlockSpec(memory_space=pltpu.VMEM)
    smem = pl.BlockSpec(memory_space=pltpu.SMEM)
    anywhere = pl.BlockSpec(memory_space=pl.ANY)
    params = pltpu.CompilerParams(vmem_limit_bytes=40 * 2**20)
    heavy = pl.CostEstimate(flops=4 * head_rows * depth * own_rows, bytes_accessed=0, transcendentals=0)
    light = pl.CostEstimate(flops=depth, bytes_accessed=0, transcendentals=0)

    def keep(x):
        return pltpu.with_memory_space_constraint(x, pltpu.VMEM)

    near_keys = passed_along(key_vectors[0, own_rows - RIM + FAR :], 1)
    scratch = [pltpu.VMEM((head_rows, WIDTH), bf16), pltpu.VMEM((tile_rows * PAIR // ROWS, WIDTH), bf16)]
    state = [
        pltpu.VMEM((task_count, head_rows, depth), bf16),
        pltpu.VMEM((task_count, depth, head_rows), bf16),
        pltpu.VMEM((task_count, head_rows, LANES), f32),
        pltpu.VMEM((task_count, tile_rows, LANES), f32),
        pltpu.VMEM((task_count, tile_rows, LANES), f32),
        pltpu.VMEM(targets.shape[1:], bf16),
        pltpu.VMEM((RIM + own_rows, depth), bf16),
        pltpu.VMEM((task_count, head_rows, depth), f32),
        pltpu.VMEM((RIM + own_rows, depth), f32),
    ]
    flipped = jnp.swapaxes(head_weights, 2, 3)
    st = pl.pallas_call(
        first_kernel,
        in_specs=[smem, smem, anywhere, vmem, vmem, vmem, anywhere, anywhere],
        out_specs=[vmem] * 10,
        out_shape=state + [pltpu.VMEM((FAR, depth), bf16)],
        scratch_shapes=scratch + [pltpu.VMEM(queries.shape[1:], bf16), pltpu.SemaphoreType.DMA((3,))],
        compiler_params=params,
        cost_estimate=heavy,
        name="own_first",
    )(tile_slot, doc_start, queries, flipped, normalizers, loss_grad, targets, key_vectors)
    fixed, moving = st[:6], st[6:9]
    far_keys = passed_along(keep(st[9]), 1)

    def piece(name, rim, moving):
        out = pl.pallas_call(
            functools.partial(piece_kernel, name),
            in_specs=[smem, smem] + [vmem] * 10,
            out_specs=[vmem] * 4,
            out_shape=state[6:] + [pltpu.VMEM((rim.shape[0] + (EXTRA if name == "near" else 0), depth), bf16)],
            input_output_aliases={9: 0, 10: 1, 11: 2},
            scratch_shapes=scratch,
            compiler_params=params,
            cost_estimate=heavy,
            name="borrowed_" + name,
        )(tile_slot, doc_start, keep(rim), *[keep(x) for x in fixed], *[keep(x) for x in moving])
        return out[:3], out[3]

    moving, near_lent = piece("near", near_keys, moving)
    near_back = passed_along(near_lent, -1)
    moving, far_lent = piece("far", far_keys, moving)
    far_back = passed_along(far_lent, -1)
    dk, q_out, w_out, k_out = pl.pallas_call(
        last_kernel,
        in_specs=[smem, smem] + [vmem] * 9,
        out_specs=[vmem, anywhere, vmem, anywhere],
        out_shape=[
            state[8],
            pltpu.HBM(queries.shape, bf16),
            jax.ShapeDtypeStruct(flipped.shape, f32),
            pltpu.HBM(key_vectors.shape, bf16),
        ],
        input_output_aliases={10: 0},
        scratch_shapes=scratch
        + [
            pltpu.VMEM((tile_rows, LANES), f32),
            pltpu.VMEM((own_rows - RIM, depth), bf16),
            pltpu.VMEM(queries.shape[1:], bf16),
            pltpu.SemaphoreType.DMA((1 + task_count,)),
        ],
        compiler_params=params,
        cost_estimate=light,
        name="own_last",
    )(tile_slot, doc_start, *[keep(x) for x in fixed], *[keep(x) for x in moving])
    k_out = pl.pallas_call(
        add_kernel,
        in_specs=[anywhere, vmem, vmem, vmem],
        out_specs=anywhere,
        out_shape=pltpu.HBM(key_vectors.shape, bf16),
        input_output_aliases={0: 0},
        scratch_shapes=[pltpu.VMEM((RIM, depth), bf16), pltpu.SemaphoreType.DMA],
        compiler_params=params,
        name="add_lent",
    )(k_out, keep(dk), keep(near_back), keep(far_back))
    return q_out, jnp.swapaxes(w_out, 2, 3), k_out


def solution(mesh):
    return jax.shard_map(
        local,
        mesh=mesh,
        in_specs=(
            P("sec", "ctx", None, None),
            P("sec", "ctx", None, None),
            P("sec", "ctx", None),
            P("sec", "ctx", None, None),
            P("sec", "ctx", None),
            P("sec", "ctx", None),
            P("sec", "ctx"),
            P("sec", "ctx"),
        ),
        out_specs=(P("sec", "ctx", None, None), P("sec", "ctx", None, None), P("sec", "ctx", None)),
        check_vma=False,
    )
```

```python
import functools

import jax
import jax.numpy as jnp
from jax import lax
from jax.experimental import pallas as pl
from jax.experimental.pallas import tpu as pltpu
from jax.sharding import PartitionSpec as P

BLK = 1024
MAXB = 4
RIM = (MAXB - 1) * BLK
FAR = RIM // 2
EXTRA = 16
WIDTH = 512
TAIL = 256
LANES = 128
ROWS = 8
PAIR = 16
DOWN = 2.0**-16
UP = 2.0**16
PRE_CHUNKS = 2
NEAR_CHUNKS = 5
FAR_CHUNKS = 3
LAST_CHUNKS = 3

f32 = jnp.float32
bf16 = jnp.bfloat16


def passed_along(array, by):
    size = lax.axis_size("ctx")
    pairs = [(i, i + by) for i in range(size) if 0 <= i + by < size]
    return lax.ppermute(array, "ctx", pairs)


def segments_of(slot_ref, doc_ref, tile_rows, own_rows):
    base = lax.axis_index("ctx") * own_rows - RIM
    out = {"far": [], "near": [], "own": []}

    def chunks(low, high):
        size = jnp.maximum(high - low, 0)
        count = (size + WIDTH - 1 - TAIL) // WIDTH
        return count, jnp.where(size > count * WIDTH, 1, 0)

    for i in range(doc_ref.shape[1]):
        doc = doc_ref[0, i] - base
        query = slot_ref[0, i] * tile_rows + RIM
        block = doc // BLK * BLK
        edge = jnp.minimum(RIM + own_rows, block + MAXB * BLK)
        end = query + tile_rows
        low = doc // LANES * LANES
        near_low = jnp.maximum(low, FAR)
        count = {"far": chunks(low, FAR), "near": chunks(near_low, RIM)}
        own_low = near_low + count["near"][0] * WIDTH + count["near"][1] * TAIL
        count["own"] = chunks(own_low, end)
        lows = {"far": low, "near": near_low, "own": own_low}
        for name in out:
            stop = jnp.int32(FAR) if name == "far" else end
            out[name].append((jnp.int32(i), lows[name], count[name][0], edge, doc, query, block, stop, count[name][1]))
    return out


def total_of(segments):
    return sum((s[2] for s in segments[1:]), segments[0][2])


def tails_of(segments):
    return sum((s[8] for s in segments[1:]), segments[0][8])


def chunk_loop(segments, skip, end, st, tails=()):
    q2, wqt, wb, nm, ct, tg, keys, dq, dk, rb, db = st
    head_rows, depth = q2.shape[1:]
    tile_rows = nm.shape[1]
    heads = head_rows // tile_rows
    rows = heads * ROWS
    blocks = tile_rows // ROWS
    factor = DOWN / depth**0.5

    def wide(x, size):
        return jnp.concatenate([x] * (size // LANES), axis=1)

    def locate(o, segments, counts, narrow):
        chosen = segments[0]
        before = jnp.int32(0)
        seen = jnp.int32(0)
        for i in range(1, len(segments)):
            seen = seen + counts[i - 1]
            later = o >= seen
            before = jnp.where(later, seen, before)
            chosen = tuple(jnp.where(later, new, old) for new, old in zip(segments[i], chosen))
        task, low, count, edge, doc, query, block, stop, _ = chosen
        size = TAIL if narrow else WIDTH
        first = low + (count if narrow else o - before) * WIDTH
        start = jnp.clip(jnp.minimum(first, edge - size), 0, keys.shape[0] - size)
        column = jnp.clip(start - block, 0, tg.shape[2] - size)
        return task, start, column, jnp.maximum(first, doc), query, stop

    def place(step):
        o = jnp.where(step >= skip[0], step + skip[1], step)
        return locate(o, segments, [s[2] for s in segments], False)

    def load(at, size):
        span = pl.ds(pl.multiple_of(at[1], LANES), size)
        return span, keys[span, :]

    def scores(b, at, key):
        size = key.shape[0]
        task, start, column, bottom, query, stop = at
        here = slice(b * rows, (b + 1) * rows)
        tile = slice(b * ROWS, (b + 1) * ROWS)
        s = lax.dot_general(
            q2[task, here, :], key, (((1,), (1,)), ((), ())), preferred_element_type=f32
        )
        r = jnp.maximum(s, 0.0)
        w = wb[task, here, :]
        index = wide(w[:ROWS], size) * r[:ROWS]
        for h in range(1, heads):
            line = slice(h * ROWS, (h + 1) * ROWS)
            index = index + wide(w[line], size) * r[line]
        rb[here, :size] = r.astype(bf16)
        target = tg[task, tile, pl.ds(pl.multiple_of(column, LANES), size)].astype(f32)
        key_row = start + lax.broadcasted_iota(jnp.int32, (ROWS, size), 1)
        query_row = query + b * ROWS + lax.broadcasted_iota(jnp.int32, (ROWS, size), 0)
        live = (key_row >= bottom) & (key_row <= jnp.minimum(query_row, stop - 1))
        delta = wide(ct[task, tile, :], size) * (jnp.exp(index - wide(nm[task, tile, :], size)) - target)
        delta = jnp.where(live, delta * factor, 0.0)
        db[b * PAIR : (b + 1) * PAIR, :size] = jnp.concatenate([delta, delta], axis=0).astype(bf16)

    def grads(b, at, key, key_sum):
        size = key.shape[0]
        here = slice(b * rows, (b + 1) * rows)
        delta = jnp.concatenate([db[b * PAIR : (b + 1) * PAIR, :size]] * (rows // PAIR), axis=0)
        grad = jnp.where(rb[here, :size] > 0, delta, jnp.zeros_like(delta))
        part = jnp.dot(wqt[at[0], :, here], grad, preferred_element_type=f32)
        key_sum = part if key_sum is None else key_sum + part
        dq[at[0], here, :] += jnp.dot(grad, key, preferred_element_type=f32)
        return key_sum

    @pl.when(end > 0)
    def _():
        at = place(jnp.int32(0))
        _, key = load(at, WIDTH)
        for b in range(blocks):
            scores(b, at, key)

        def body(step, old):
            at = place(step)
            span, old_key = load(old, WIDTH)
            _, key = load(at, WIDTH)
            key_sum = None
            for b in range(blocks):
                key_sum = grads(b, old, old_key, key_sum)
                scores(b, at, key)
            dk[span, :] += key_sum.T
            return at

        at = lax.fori_loop(1, end, body, at)
        span, key = load(at, WIDTH)
        key_sum = None
        for b in range(blocks):
            key_sum = grads(b, at, key, key_sum)
        dk[span, :] += key_sum.T

    if not tails:
        return

    def narrow(step, carry):
        at = locate(step, tails, [s[8] for s in tails], True)
        span, key = load(at, TAIL)
        for b in range(blocks):
            scores(b, at, key)
        key_sum = None
        for b in range(blocks):
            key_sum = grads(b, at, key, key_sum)
        dk[span, :] += key_sum.T
        return carry

    lax.fori_loop(0, tails_of(tails), narrow, jnp.int32(0))


def plan(slot, doc, tile_rows, own_rows):
    segments = segments_of(slot, doc, tile_rows, own_rows)
    near = total_of(segments["near"])
    far = total_of(segments["far"])
    own = total_of(segments["own"])
    one = jnp.minimum(own, PRE_CHUNKS)
    rest = jnp.maximum(own - one - LAST_CHUNKS, 0)
    near_room = jnp.maximum(NEAR_CHUNKS - near - tails_of(segments["near"]), 0)
    far_room = jnp.maximum(FAR_CHUNKS - far - tails_of(segments["far"]), 0)
    near_fill = jnp.minimum((rest + 1) // 2, near_room)
    far_fill = jnp.minimum(rest - near_fill, far_room)
    two = one + near_fill
    three = two + far_fill
    return segments, near, far, (jnp.int32(0), one, two, three, own)


def first_kernel(slot, doc, q, w, nrm, cot, tgt, key, q2, wqt, wb, nm, ct, tg, keys, dq, dk, far, rb, db, q_in, sems):
    own_rows = key.shape[1]
    copies = [
        pltpu.make_async_copy(q.at[0], q_in, sems.at[0]),
        pltpu.make_async_copy(key.at[0], keys.at[RIM : RIM + own_rows], sems.at[1]),
        pltpu.make_async_copy(tgt.at[0], tg, sems.at[2]),
    ]
    for copy in copies:
        copy.start()
    heads, tile_rows = w.shape[2:]
    depth = q2.shape[2]
    rows = heads * ROWS
    blocks = tile_rows // ROWS
    turn = LANES // ROWS
    dq[...] = jnp.zeros_like(dq)
    dk[...] = jnp.zeros_like(dk)
    for i in range(w.shape[1]):
        plain = w[0, i].T * (1.0 / depth**0.5)
        nm[i] = jnp.broadcast_to(nrm[0, i : i + 1, :], (LANES, tile_rows)).T
        ct[i] = jnp.broadcast_to(cot[0, i : i + 1, :], (LANES, tile_rows)).T
        for h in range(heads):
            column = jnp.broadcast_to(plain[:, h : h + 1], (tile_rows, LANES))
            for b in range(blocks):
                wb[i, b * rows + h * ROWS : b * rows + (h + 1) * ROWS, :] = column[b * ROWS : (b + 1) * ROWS]
    copies[0].wait()
    for i in range(w.shape[1]):
        for h in range(0, heads, turn):
            queries = [q_in[i, :, u * depth : (u + 1) * depth].astype(f32) for u in range(h, h + turn)]
            for b in range(blocks):
                here = slice(b * rows + h * ROWS, b * rows + (h + turn) * ROWS)
                some = jnp.concatenate([x[b * ROWS : (b + 1) * ROWS] for x in queries], axis=0)
                q2[i, here, :] = some.astype(bf16)
                wqt[i, :, here] = (some * wb[i, here, :]).astype(bf16).T
    copies[1].wait()
    copies[2].wait()
    far[...] = keys[own_rows : own_rows + FAR, :]
    segments, _, _, marks = plan(slot, doc, tile_rows, own_rows)
    chunk_loop(segments["own"], (marks[1], 0), marks[1], (q2, wqt, wb, nm, ct, tg, keys, dq, dk, rb, db))


def piece_kernel(name, slot, doc, rim, q2, wqt, wb, nm, ct, tg, *refs):
    keys, dq, dk, lent, rb, db = refs[3:]
    tile_rows = nm.shape[1]
    start, stop = (FAR, RIM) if name == "near" else (0, FAR)
    keys[start:stop, :] = rim[...]
    segments, near, far, marks = plan(slot, doc, tile_rows, keys.shape[0] - RIM)
    count, at = (near, 1) if name == "near" else (far, 2)
    st = (q2, wqt, wb, nm, ct, tg, keys, dq, dk, rb, db)
    chunk_loop(segments[name] + segments["own"], (count, marks[at]), count + marks[at + 1] - marks[at], st, segments[name])
    lent[: stop - start, :] = (dk[start:stop, :] * (UP * q2.shape[2] ** 0.5)).astype(bf16)
    if name == "near":
        lent[stop - start :, :] = jnp.zeros((EXTRA, lent.shape[1]), bf16)


def last_kernel(slot, doc, q2, wqt, wb, nm, ct, tg, keys, dq, dk_in, *refs):
    dk, q_out, w_out, k_out, rb, db, dots, whole, full_q, sems = refs
    tile_rows = nm.shape[1]
    head_rows, depth = q2.shape[1:]
    heads = head_rows // tile_rows
    rows = heads * ROWS
    own_rows = keys.shape[0] - RIM
    segments, _, _, marks = plan(slot, doc, tile_rows, own_rows)
    st = (q2, wqt, wb, nm, ct, tg, keys, dq, dk, rb, db)
    chunk_loop(segments["own"], (0, marks[3]), marks[4] - marks[3], st, segments["own"])
    copies = []
    for i in range(q2.shape[0]):
        for b in range(0, tile_rows // ROWS, 2):
            for h in range(0, heads, 2):
                full = []
                for c in range(2):
                    at = (b + c) * rows + h * ROWS
                    full.append(dq[i, at : at + PAIR, :] * (wb[i, at : at + PAIR, :] * (UP * depth**0.5)))
                for u in range(2):
                    line = slice(u * ROWS, (u + 1) * ROWS)
                    full_q[i, b * ROWS : (b + 2) * ROWS, (h + u) * depth : (h + u + 1) * depth] = (
                        jnp.concatenate([full[0][line], full[1][line]], axis=0).astype(bf16)
                    )
        copies.append(pltpu.make_async_copy(full_q.at[i], q_out.at[0, i], sems.at[i]))
        copies[-1].start()
    settled = own_rows - RIM
    whole[...] = (dk[RIM : RIM + settled, :] * (UP * depth**0.5)).astype(bf16)
    copies.append(pltpu.make_async_copy(whole, k_out.at[0, :settled], sems.at[q2.shape[0]]))
    copies[-1].start()
    lane = lax.broadcasted_iota(jnp.int32, (ROWS, LANES), 1)
    for i in range(q2.shape[0]):
        for b in range(tile_rows // ROWS):
            sums = jnp.zeros((ROWS, LANES), f32)
            for h in range(0, heads, 2):
                at = slice(b * rows + h * ROWS, b * rows + h * ROWS + PAIR)
                dot = dq[i, at, :] * q2[i, at, :].astype(f32)
                for u in range(2):
                    line = slice(u * ROWS, (u + 1) * ROWS)
                    sums = jnp.where(lane == h + u, jnp.sum(dot[line], axis=1, keepdims=True), sums)
            dots[b * ROWS : (b + 1) * ROWS, :] = sums * UP
        w_out[0, i] = dots[:, :heads].T
    for copy in copies:
        copy.wait()


def add_kernel(k_in, dk, near, far, k_out, tail, sem):
    own_rows = k_out.shape[1]
    own = dk[own_rows:, :] * (UP * dk.shape[1] ** 0.5)
    tail[:FAR] = (own[:FAR] + far[...].astype(f32)).astype(bf16)
    tail[FAR:] = (own[FAR:] + near[: RIM - FAR].astype(f32)).astype(bf16)
    copy = pltpu.make_async_copy(tail, k_out.at[0, own_rows - RIM :], sem)
    copy.start()
    copy.wait()


def local(queries, head_weights, key_vectors, targets, normalizers, loss_grad, tile_slot, doc_start):
    task_count, tile_rows, width = queries.shape[1:]
    heads = head_weights.shape[3]
    own_rows, depth = key_vectors.shape[1:]
    head_rows = heads * tile_rows
    vmem = pl.BlockSpec(memory_space=pltpu.VMEM)
    smem = pl.BlockSpec(memory_space=pltpu.SMEM)
    anywhere = pl.BlockSpec(memory_space=pl.ANY)
    params = pltpu.CompilerParams(vmem_limit_bytes=40 * 2**20)
    heavy = pl.CostEstimate(flops=4 * head_rows * depth * own_rows, bytes_accessed=0, transcendentals=0)
    light = pl.CostEstimate(flops=depth, bytes_accessed=0, transcendentals=0)

    def keep(x):
        return pltpu.with_memory_space_constraint(x, pltpu.VMEM)

    near_keys = passed_along(key_vectors[0, own_rows - RIM + FAR :], 1)
    scratch = [pltpu.VMEM((head_rows, WIDTH), bf16), pltpu.VMEM((tile_rows * PAIR // ROWS, WIDTH), bf16)]
    state = [
        pltpu.VMEM((task_count, head_rows, depth), bf16),
        pltpu.VMEM((task_count, depth, head_rows), bf16),
        pltpu.VMEM((task_count, head_rows, LANES), f32),
        pltpu.VMEM((task_count, tile_rows, LANES), f32),
        pltpu.VMEM((task_count, tile_rows, LANES), f32),
        pltpu.VMEM(targets.shape[1:], bf16),
        pltpu.VMEM((RIM + own_rows, depth), bf16),
        pltpu.VMEM((task_count, head_rows, depth), f32),
        pltpu.VMEM((RIM + own_rows, depth), f32),
    ]
    flipped = jnp.swapaxes(head_weights, 2, 3)
    st = pl.pallas_call(
        first_kernel,
        in_specs=[smem, smem, anywhere, vmem, vmem, vmem, anywhere, anywhere],
        out_specs=[vmem] * 10,
        out_shape=state + [pltpu.VMEM((FAR, depth), bf16)],
        scratch_shapes=scratch + [pltpu.VMEM(queries.shape[1:], bf16), pltpu.SemaphoreType.DMA((3,))],
        compiler_params=params,
        cost_estimate=heavy,
        name="own_first",
    )(tile_slot, doc_start, queries, flipped, normalizers, loss_grad, targets, key_vectors)
    fixed, moving = st[:6], st[6:9]
    far_keys = passed_along(keep(st[9]), 1)

    def piece(name, rim, moving):
        out = pl.pallas_call(
            functools.partial(piece_kernel, name),
            in_specs=[smem, smem] + [vmem] * 10,
            out_specs=[vmem] * 4,
            out_shape=state[6:] + [pltpu.VMEM((rim.shape[0] + (EXTRA if name == "near" else 0), depth), bf16)],
            input_output_aliases={9: 0, 10: 1, 11: 2},
            scratch_shapes=scratch,
            compiler_params=params,
            cost_estimate=heavy,
            name="borrowed_" + name,
        )(tile_slot, doc_start, keep(rim), *[keep(x) for x in fixed], *[keep(x) for x in moving])
        return out[:3], out[3]

    moving, near_lent = piece("near", near_keys, moving)
    near_back = passed_along(near_lent, -1)
    moving, far_lent = piece("far", far_keys, moving)
    far_back = passed_along(far_lent, -1)
    dk, q_out, w_out, k_out = pl.pallas_call(
        last_kernel,
        in_specs=[smem, smem] + [vmem] * 9,
        out_specs=[vmem, anywhere, vmem, anywhere],
        out_shape=[
            state[8],
            pltpu.HBM(queries.shape, bf16),
            jax.ShapeDtypeStruct(flipped.shape, f32),
            pltpu.HBM(key_vectors.shape, bf16),
        ],
        input_output_aliases={10: 0},
        scratch_shapes=scratch
        + [
            pltpu.VMEM((tile_rows, LANES), f32),
            pltpu.VMEM((own_rows - RIM, depth), bf16),
            pltpu.VMEM(queries.shape[1:], bf16),
            pltpu.SemaphoreType.DMA((1 + task_count,)),
        ],
        compiler_params=params,
        cost_estimate=light,
        name="own_last",
    )(tile_slot, doc_start, *[keep(x) for x in fixed], *[keep(x) for x in moving])
    k_out = pl.pallas_call(
        add_kernel,
        in_specs=[anywhere, vmem, vmem, vmem],
        out_specs=anywhere,
        out_shape=pltpu.HBM(key_vectors.shape, bf16),
        input_output_aliases={0: 0},
        scratch_shapes=[pltpu.VMEM((RIM, depth), bf16), pltpu.SemaphoreType.DMA],
        compiler_params=params,
        name="add_lent",
    )(k_out, keep(dk), keep(near_back), keep(far_back))
    return q_out, jnp.swapaxes(w_out, 2, 3), k_out


def solution(mesh):
    return jax.shard_map(
        local,
        mesh=mesh,
        in_specs=(
            P("sec", "ctx", None, None),
            P("sec", "ctx", None, None),
            P("sec", "ctx", None),
            P("sec", "ctx", None, None),
            P("sec", "ctx", None),
            P("sec", "ctx", None),
            P("sec", "ctx"),
            P("sec", "ctx"),
        ),
        out_specs=(P("sec", "ctx", None, None), P("sec", "ctx", None, None), P("sec", "ctx", None)),
        check_vma=False,
    )
```

```python
import functools

import jax
import jax.numpy as jnp
from jax import lax
from jax.experimental import pallas as pl
from jax.experimental.pallas import tpu as pltpu
from jax.sharding import PartitionSpec as P

BLK = 1024
MAXB = 4
RIM = (MAXB - 1) * BLK
FAR = RIM // 2
EXTRA = 16
WIDTH = 512
TAIL = 256
LANES = 128
ROWS = 8
PAIR = 16
DOWN = 2.0**-16
UP = 2.0**16
PRE_CHUNKS = 2
NEAR_CHUNKS = 5
FAR_CHUNKS = 3
LAST_CHUNKS = 3

f32 = jnp.float32
bf16 = jnp.bfloat16


def passed_along(array, by):
    size = lax.axis_size("ctx")
    pairs = [(i, i + by) for i in range(size) if 0 <= i + by < size]
    return lax.ppermute(array, "ctx", pairs)


def segments_of(slot_ref, doc_ref, tile_rows, own_rows):
    base = lax.axis_index("ctx") * own_rows - RIM
    out = {"far": [], "near": [], "own": []}

    def chunks(low, high):
        size = jnp.maximum(high - low, 0)
        count = (size + WIDTH - 1 - TAIL) // WIDTH
        return count, jnp.where(size > count * WIDTH, 1, 0)

    for i in range(doc_ref.shape[1]):
        doc = doc_ref[0, i] - base
        query = slot_ref[0, i] * tile_rows + RIM
        block = doc // BLK * BLK
        edge = jnp.minimum(RIM + own_rows, block + MAXB * BLK)
        end = query + tile_rows
        low = doc // LANES * LANES
        near_low = jnp.maximum(low, FAR)
        count = {"far": chunks(low, FAR), "near": chunks(near_low, RIM)}
        own_low = near_low + count["near"][0] * WIDTH + count["near"][1] * TAIL
        count["own"] = chunks(own_low, end)
        lows = {"far": low, "near": near_low, "own": own_low}
        for name in out:
            stop = jnp.int32(FAR) if name == "far" else end
            out[name].append((jnp.int32(i), lows[name], count[name][0], edge, doc, query, block, stop, count[name][1]))
    return out


def total_of(segments):
    return sum((s[2] for s in segments[1:]), segments[0][2])


def tails_of(segments):
    return sum((s[8] for s in segments[1:]), segments[0][8])


def chunk_loop(segments, skip, end, st, tails=()):
    q2, wqt, wb, nm, ct, tg, keys, dq, dk, rb, db = st
    head_rows, depth = q2.shape[1:]
    tile_rows = nm.shape[1]
    heads = head_rows // tile_rows
    rows = heads * ROWS
    blocks = tile_rows // ROWS
    factor = DOWN / depth**0.5

    def wide(x, size):
        return jnp.concatenate([x] * (size // LANES), axis=1)

    def locate(o, segments, counts, narrow):
        chosen = segments[0]
        before = jnp.int32(0)
        seen = jnp.int32(0)
        for i in range(1, len(segments)):
            seen = seen + counts[i - 1]
            later = o >= seen
            before = jnp.where(later, seen, before)
            chosen = tuple(jnp.where(later, new, old) for new, old in zip(segments[i], chosen))
        task, low, count, edge, doc, query, block, stop, _ = chosen
        size = TAIL if narrow else WIDTH
        first = low + (count if narrow else o - before) * WIDTH
        start = jnp.clip(jnp.minimum(first, edge - size), 0, keys.shape[0] - size)
        column = jnp.clip(start - block, 0, tg.shape[2] - size)
        return task, start, column, jnp.maximum(first, doc), query, stop

    def place(step):
        o = jnp.where(step >= skip[0], step + skip[1], step)
        return locate(o, segments, [s[2] for s in segments], False)

    def load(at, size):
        span = pl.ds(pl.multiple_of(at[1], LANES), size)
        return span, keys[span, :]

    def scores(b, at, key):
        size = key.shape[0]
        task, start, column, bottom, query, stop = at
        here = slice(b * rows, (b + 1) * rows)
        tile = slice(b * ROWS, (b + 1) * ROWS)
        s = lax.dot_general(
            q2[task, here, :], key, (((1,), (1,)), ((), ())), preferred_element_type=f32
        )
        r = jnp.maximum(s, 0.0)
        w = wb[task, here, :]
        index = wide(w[:ROWS], size) * r[:ROWS]
        for h in range(1, heads):
            line = slice(h * ROWS, (h + 1) * ROWS)
            index = index + wide(w[line], size) * r[line]
        rb[here, :size] = r.astype(bf16)
        target = tg[task, tile, pl.ds(pl.multiple_of(column, LANES), size)].astype(f32)
        key_row = start + lax.broadcasted_iota(jnp.int32, (ROWS, size), 1)
        query_row = query + b * ROWS + lax.broadcasted_iota(jnp.int32, (ROWS, size), 0)
        live = (key_row >= bottom) & (key_row <= jnp.minimum(query_row, stop - 1))
        delta = wide(ct[task, tile, :], size) * (jnp.exp(index - wide(nm[task, tile, :], size)) - target)
        delta = jnp.where(live, delta * factor, 0.0)
        db[b * PAIR : (b + 1) * PAIR, :size] = jnp.concatenate([delta, delta], axis=0).astype(bf16)

    def grads(b, at, key, key_sum):
        size = key.shape[0]
        here = slice(b * rows, (b + 1) * rows)
        delta = jnp.concatenate([db[b * PAIR : (b + 1) * PAIR, :size]] * (rows // PAIR), axis=0)
        grad = jnp.where(rb[here, :size] > 0, delta, jnp.zeros_like(delta))
        part = jnp.dot(wqt[at[0], :, here], grad, preferred_element_type=f32)
        key_sum = part if key_sum is None else key_sum + part
        dq[at[0], here, :] += jnp.dot(grad, key, preferred_element_type=f32)
        return key_sum

    @pl.when(end > 0)
    def _():
        at = place(jnp.int32(0))
        _, key = load(at, WIDTH)
        for b in range(blocks):
            scores(b, at, key)

        def body(step, old):
            at = place(step)
            span, old_key = load(old, WIDTH)
            _, key = load(at, WIDTH)
            key_sum = None
            for b in range(blocks):
                key_sum = grads(b, old, old_key, key_sum)
                scores(b, at, key)
            dk[span, :] += key_sum.T
            return at

        at = lax.fori_loop(1, end, body, at)
        span, key = load(at, WIDTH)
        key_sum = None
        for b in range(blocks):
            key_sum = grads(b, at, key, key_sum)
        dk[span, :] += key_sum.T

    if not tails:
        return

    def narrow(step, carry):
        at = locate(step, tails, [s[8] for s in tails], True)
        span, key = load(at, TAIL)
        for b in range(blocks):
            scores(b, at, key)
        key_sum = None
        for b in range(blocks):
            key_sum = grads(b, at, key, key_sum)
        dk[span, :] += key_sum.T
        return carry

    lax.fori_loop(0, tails_of(tails), narrow, jnp.int32(0))


def plan(slot, doc, tile_rows, own_rows):
    segments = segments_of(slot, doc, tile_rows, own_rows)
    near = total_of(segments["near"])
    far = total_of(segments["far"])
    own = total_of(segments["own"])
    one = jnp.minimum(own, PRE_CHUNKS)
    rest = jnp.maximum(own - one - LAST_CHUNKS, 0)
    near_room = jnp.maximum(NEAR_CHUNKS - near - tails_of(segments["near"]), 0)
    far_room = jnp.maximum(FAR_CHUNKS - far - tails_of(segments["far"]), 0)
    near_fill = jnp.minimum((rest + 1) // 2, near_room)
    far_fill = jnp.minimum(rest - near_fill, far_room)
    two = one + near_fill
    three = two + far_fill
    return segments, near, far, (jnp.int32(0), one, two, three, own)


def first_kernel(slot, doc, q, w, nrm, cot, tgt, key, q2, wqt, wb, nm, ct, tg, keys, dq, dk, far, rb, db, q_in, sems):
    own_rows = key.shape[1]
    copies = [
        pltpu.make_async_copy(q.at[0], q_in, sems.at[0]),
        pltpu.make_async_copy(key.at[0], keys.at[RIM : RIM + own_rows], sems.at[1]),
        pltpu.make_async_copy(tgt.at[0], tg, sems.at[2]),
    ]
    for copy in copies:
        copy.start()
    heads, tile_rows = w.shape[2:]
    depth = q2.shape[2]
    rows = heads * ROWS
    blocks = tile_rows // ROWS
    turn = LANES // ROWS
    dq[...] = jnp.zeros_like(dq)
    dk[...] = jnp.zeros_like(dk)
    for i in range(w.shape[1]):
        plain = w[0, i].T * (1.0 / depth**0.5)
        nm[i] = jnp.broadcast_to(nrm[0, i : i + 1, :], (LANES, tile_rows)).T
        ct[i] = jnp.broadcast_to(cot[0, i : i + 1, :], (LANES, tile_rows)).T
        for h in range(heads):
            column = jnp.broadcast_to(plain[:, h : h + 1], (tile_rows, LANES))
            for b in range(blocks):
                wb[i, b * rows + h * ROWS : b * rows + (h + 1) * ROWS, :] = column[b * ROWS : (b + 1) * ROWS]
    copies[0].wait()
    for i in range(w.shape[1]):
        for h in range(0, heads, turn):
            queries = [q_in[i, :, u * depth : (u + 1) * depth].astype(f32) for u in range(h, h + turn)]
            for b in range(blocks):
                here = slice(b * rows + h * ROWS, b * rows + (h + turn) * ROWS)
                some = jnp.concatenate([x[b * ROWS : (b + 1) * ROWS] for x in queries], axis=0)
                q2[i, here, :] = some.astype(bf16)
                wqt[i, :, here] = (some * wb[i, here, :]).astype(bf16).T
    copies[1].wait()
    copies[2].wait()
    far[...] = keys[own_rows : own_rows + FAR, :]
    segments, _, _, marks = plan(slot, doc, tile_rows, own_rows)
    chunk_loop(segments["own"], (marks[1], 0), marks[1], (q2, wqt, wb, nm, ct, tg, keys, dq, dk, rb, db))


def piece_kernel(name, slot, doc, rim, q2, wqt, wb, nm, ct, tg, *refs):
    keys, dq, dk, lent, rb, db = refs[3:]
    tile_rows = nm.shape[1]
    start, stop = (FAR, RIM) if name == "near" else (0, FAR)
    keys[start:stop, :] = rim[...]
    segments, near, far, marks = plan(slot, doc, tile_rows, keys.shape[0] - RIM)
    count, at = (near, 1) if name == "near" else (far, 2)
    st = (q2, wqt, wb, nm, ct, tg, keys, dq, dk, rb, db)
    chunk_loop(segments[name] + segments["own"], (count, marks[at]), count + marks[at + 1] - marks[at], st, segments[name])
    lent[: stop - start, :] = (dk[start:stop, :] * (UP * q2.shape[2] ** 0.5)).astype(bf16)
    if name == "near":
        lent[stop - start :, :] = jnp.zeros((EXTRA, lent.shape[1]), bf16)


def last_kernel(slot, doc, q2, wqt, wb, nm, ct, tg, keys, dq, dk_in, *refs):
    dk, q_out, w_out, k_out, rb, db, dots, whole, full_q, sems = refs
    tile_rows = nm.shape[1]
    head_rows, depth = q2.shape[1:]
    heads = head_rows // tile_rows
    rows = heads * ROWS
    own_rows = keys.shape[0] - RIM
    segments, _, _, marks = plan(slot, doc, tile_rows, own_rows)
    st = (q2, wqt, wb, nm, ct, tg, keys, dq, dk, rb, db)
    chunk_loop(segments["own"], (0, marks[3]), marks[4] - marks[3], st, segments["own"])
    copies = []
    for i in range(q2.shape[0]):
        for b in range(0, tile_rows // ROWS, 2):
            for h in range(0, heads, 2):
                full = []
                for c in range(2):
                    at = (b + c) * rows + h * ROWS
                    full.append(dq[i, at : at + PAIR, :] * (wb[i, at : at + PAIR, :] * (UP * depth**0.5)))
                for u in range(2):
                    line = slice(u * ROWS, (u + 1) * ROWS)
                    full_q[i, b * ROWS : (b + 2) * ROWS, (h + u) * depth : (h + u + 1) * depth] = (
                        jnp.concatenate([full[0][line], full[1][line]], axis=0).astype(bf16)
                    )
        copies.append(pltpu.make_async_copy(full_q.at[i], q_out.at[0, i], sems.at[i]))
        copies[-1].start()
    settled = own_rows - RIM
    whole[...] = (dk[RIM : RIM + settled, :] * (UP * depth**0.5)).astype(bf16)
    copies.append(pltpu.make_async_copy(whole, k_out.at[0, :settled], sems.at[q2.shape[0]]))
    copies[-1].start()
    lane = lax.broadcasted_iota(jnp.int32, (ROWS, LANES), 1)
    for i in range(q2.shape[0]):
        for b in range(tile_rows // ROWS):
            sums = jnp.zeros((ROWS, LANES), f32)
            for h in range(0, heads, 2):
                at = slice(b * rows + h * ROWS, b * rows + h * ROWS + PAIR)
                dot = dq[i, at, :] * q2[i, at, :].astype(f32)
                for u in range(2):
                    line = slice(u * ROWS, (u + 1) * ROWS)
                    sums = jnp.where(lane == h + u, jnp.sum(dot[line], axis=1, keepdims=True), sums)
            dots[b * ROWS : (b + 1) * ROWS, :] = sums * UP
        w_out[0, i] = dots[:, :heads].T
    for copy in copies:
        copy.wait()


def add_kernel(k_in, dk, near, far, k_out, tail, sems):
    own_rows = k_out.shape[1]
    own = dk[own_rows:, :] * (UP * dk.shape[1] ** 0.5)
    first = own_rows - RIM
    tail[FAR:] = (own[FAR:] + near[: RIM - FAR].astype(f32)).astype(bf16)
    copies = [pltpu.make_async_copy(tail.at[FAR:], k_out.at[0, first + FAR :], sems.at[0])]
    copies[0].start()
    tail[:FAR] = (own[:FAR] + far[...].astype(f32)).astype(bf16)
    copies.append(pltpu.make_async_copy(tail.at[:FAR], k_out.at[0, first : first + FAR], sems.at[1]))
    copies[1].start()
    for copy in copies:
        copy.wait()


def local(queries, head_weights, key_vectors, targets, normalizers, loss_grad, tile_slot, doc_start):
    task_count, tile_rows, width = queries.shape[1:]
    heads = head_weights.shape[3]
    own_rows, depth = key_vectors.shape[1:]
    head_rows = heads * tile_rows
    vmem = pl.BlockSpec(memory_space=pltpu.VMEM)
    smem = pl.BlockSpec(memory_space=pltpu.SMEM)
    anywhere = pl.BlockSpec(memory_space=pl.ANY)
    params = pltpu.CompilerParams(vmem_limit_bytes=40 * 2**20)
    heavy = pl.CostEstimate(flops=4 * head_rows * depth * own_rows, bytes_accessed=0, transcendentals=0)
    light = pl.CostEstimate(flops=depth, bytes_accessed=0, transcendentals=0)

    def keep(x):
        return pltpu.with_memory_space_constraint(x, pltpu.VMEM)

    near_keys = passed_along(key_vectors[0, own_rows - RIM + FAR :], 1)
    scratch = [pltpu.VMEM((head_rows, WIDTH), bf16), pltpu.VMEM((tile_rows * PAIR // ROWS, WIDTH), bf16)]
    state = [
        pltpu.VMEM((task_count, head_rows, depth), bf16),
        pltpu.VMEM((task_count, depth, head_rows), bf16),
        pltpu.VMEM((task_count, head_rows, LANES), f32),
        pltpu.VMEM((task_count, tile_rows, LANES), f32),
        pltpu.VMEM((task_count, tile_rows, LANES), f32),
        pltpu.VMEM(targets.shape[1:], bf16),
        pltpu.VMEM((RIM + own_rows, depth), bf16),
        pltpu.VMEM((task_count, head_rows, depth), f32),
        pltpu.VMEM((RIM + own_rows, depth), f32),
    ]
    flipped = jnp.swapaxes(head_weights, 2, 3)
    st = pl.pallas_call(
        first_kernel,
        in_specs=[smem, smem, anywhere, vmem, vmem, vmem, anywhere, anywhere],
        out_specs=[vmem] * 10,
        out_shape=state + [pltpu.VMEM((FAR, depth), bf16)],
        scratch_shapes=scratch + [pltpu.VMEM(queries.shape[1:], bf16), pltpu.SemaphoreType.DMA((3,))],
        compiler_params=params,
        cost_estimate=heavy,
        name="own_first",
    )(tile_slot, doc_start, queries, flipped, normalizers, loss_grad, targets, key_vectors)
    fixed, moving = st[:6], st[6:9]
    far_keys = passed_along(keep(st[9]), 1)

    def piece(name, rim, moving):
        out = pl.pallas_call(
            functools.partial(piece_kernel, name),
            in_specs=[smem, smem] + [vmem] * 10,
            out_specs=[vmem] * 4,
            out_shape=state[6:] + [pltpu.VMEM((rim.shape[0] + (EXTRA if name == "near" else 0), depth), bf16)],
            input_output_aliases={9: 0, 10: 1, 11: 2},
            scratch_shapes=scratch,
            compiler_params=params,
            cost_estimate=heavy,
            name="borrowed_" + name,
        )(tile_slot, doc_start, keep(rim), *[keep(x) for x in fixed], *[keep(x) for x in moving])
        return out[:3], out[3]

    moving, near_lent = piece("near", near_keys, moving)
    near_back = passed_along(near_lent, -1)
    moving, far_lent = piece("far", far_keys, moving)
    far_back = passed_along(far_lent, -1)
    dk, q_out, w_out, k_out = pl.pallas_call(
        last_kernel,
        in_specs=[smem, smem] + [vmem] * 9,
        out_specs=[vmem, anywhere, vmem, anywhere],
        out_shape=[
            state[8],
            pltpu.HBM(queries.shape, bf16),
            jax.ShapeDtypeStruct(flipped.shape, f32),
            pltpu.HBM(key_vectors.shape, bf16),
        ],
        input_output_aliases={10: 0},
        scratch_shapes=scratch
        + [
            pltpu.VMEM((tile_rows, LANES), f32),
            pltpu.VMEM((own_rows - RIM, depth), bf16),
            pltpu.VMEM(queries.shape[1:], bf16),
            pltpu.SemaphoreType.DMA((1 + task_count,)),
        ],
        compiler_params=params,
        cost_estimate=light,
        name="own_last",
    )(tile_slot, doc_start, *[keep(x) for x in fixed], *[keep(x) for x in moving])
    k_out = pl.pallas_call(
        add_kernel,
        in_specs=[anywhere, vmem, vmem, vmem],
        out_specs=anywhere,
        out_shape=pltpu.HBM(key_vectors.shape, bf16),
        input_output_aliases={0: 0},
        scratch_shapes=[pltpu.VMEM((RIM, depth), bf16), pltpu.SemaphoreType.DMA((2,))],
        compiler_params=params,
        name="add_lent",
    )(k_out, keep(dk), keep(near_back), keep(far_back))
    return q_out, jnp.swapaxes(w_out, 2, 3), k_out


def solution(mesh):
    return jax.shard_map(
        local,
        mesh=mesh,
        in_specs=(
            P("sec", "ctx", None, None),
            P("sec", "ctx", None, None),
            P("sec", "ctx", None),
            P("sec", "ctx", None, None),
            P("sec", "ctx", None),
            P("sec", "ctx", None),
            P("sec", "ctx"),
            P("sec", "ctx"),
        ),
        out_specs=(P("sec", "ctx", None, None), P("sec", "ctx", None, None), P("sec", "ctx", None)),
        check_vma=False,
    )
```
